256 devices in a mesh: row: 16 (over x_hi, y, core), col: 16 (over z, x_lo).
Axes of the slice: x: 4 (x_hi: 2, x_lo: 2; x = x_hi * 2 + x_lo), y: 4, z: 8, core: 2. Of those that a mesh axis runs over, the one named last changes fastest.
Arguments:
- points: bfloat16 [24576, 768], P('row'), may hold values from -16 to 16
Outputs:
- density: float32 [24576], P(('row', 'col'))
- recon: float32 [24576, 768], P(('row', 'col'))
The draws below stay inside these ranges and needn't reach their ends.
All inputs are finite; a program needn't handle non-finite values.
Results may differ from the reference program's by a relative error of at most 0.0014.
Values may be sent and summed in bfloat16 or wider, within the bound.
A program may use at most 64 MiB of HBM per device.

```python
import math
import jax
import jax.numpy as jnp
from jax import lax

D = 768
PTS_DEV = 96
POINTS = 24576


def draw_points(key, part):
    key = jax.random.fold_in(key, 7)
    key_base = jax.random.fold_in(key, 0)
    base = jax.random.normal(key_base, (POINTS, D), jnp.float32)
    field = jnp.clip(base, -6.0, 6.0)
    return field.astype(jnp.bfloat16)


def setup_inputs(seed: int = 0) -> dict:
    key_list = jax.random.split(jax.random.key(seed), 2)
    points = draw_points(jax.random.fold_in(key_list[1], 71), 0)
    return dict(points=points)


NEG = -1e+30

def assigned(first_ids, second_ids, span):
    first_stretch = first_ids[:, None] // span
    second_stretch = second_ids[None, :] // span
    parity = (first_stretch + second_stretch) % 2
    same = (first_stretch == second_stretch) & (first_ids[:, None] < second_ids[None, :])
    above = (first_stretch < second_stretch) & (parity == 0)
    below = (first_stretch > second_stretch) & (parity == 1)
    return same | above | below

def one_side(scores, mask, points):
    top = lax.optimization_barrier(jnp.max(jnp.where(mask, scores, NEG), axis=1))
    weights = jnp.where(mask, jnp.exp(scores - top[:, None]), 0.0).astype(jnp.bfloat16)
    total = lax.optimization_barrier(jnp.sum(weights, axis=1, dtype=jnp.float32))
    mixed = jnp.dot(weights, points, preferred_element_type=jnp.float32)
    return (top, total, mixed)

def combine(row_top, row_sum, row_mix, col_top, col_sum, col_mix):
    top = jnp.maximum(row_top, col_top)
    row_factor = jnp.exp(row_top - top)
    col_factor = jnp.exp(col_top - top)
    total = row_sum * row_factor + col_sum * col_factor
    density = top + jnp.log(total)
    recon = (row_mix * row_factor[:, None] + col_mix * col_factor[:, None]) / total[:, None]
    return (density, recon)

def reference(points):
    count = points.shape[0]
    block = math.gcd(count, 1024)
    scale = 1.0 / math.sqrt(D)
    all_ids = jnp.arange(count, dtype=jnp.int32)

    def one_block(start):
        rows = lax.dynamic_slice_in_dim(points, start, block, 0)
        ids = start + jnp.arange(block, dtype=jnp.int32)
        scores = lax.dot_general(rows, points, (((1,), (1,)), ((), ())), preferred_element_type=jnp.float32) * scale
        row_top, row_sum, row_mix = one_side(scores, assigned(ids, all_ids, PTS_DEV), points)
        col_top, col_sum, col_mix = one_side(scores, assigned(all_ids, ids, PTS_DEV).T, points)
        return combine(row_top, row_sum, row_mix, col_top, col_sum, col_mix)
    starts = jnp.arange(0, count, block, dtype=jnp.int32)
    density, recon = lax.map(one_block, starts)
    return (density.reshape(count), recon.reshape(count, D))
```

```python
import functools
import math

import jax
import jax.numpy as jnp
from jax import lax
from jax.experimental import pallas as pl
from jax.experimental.pallas import tpu as pltpu
from jax.sharding import PartitionSpec as P

MESH = pl.DeviceIdType.MESH
NEG = -1e30
LOG2E = math.log2(math.e)
LN2 = math.log(2.0)

NX, NY, NZ = 4, 4, 8
STEPS = (
    ((0, 0), (1, 0), (-1, 0), (0, 1), (0, -1)),
    ((1, 1), (1, -1), (-1, 1), (-1, -1)),
    ((2, 0), (0, 2)),
    ((1, 2), (-1, 2), (2, 1), (2, -1), (2, 2)),
)
ORDER = (4, 3, -3, 2, -2, 1, -1, 0)
DIRS = {"x+": (1, 0), "x-": (-1, 0), "y+": (0, 1), "y-": (0, -1)}


def wrap(v):
    v %= 4
    return v - 4 if v == 3 else v


def kernel(span, points, recon, density, keys, queries, acc, tops, sums, own_stats,
           in_mix, out_mix, in_last, out_last, in_stats, out_stats,
           load_sem, send_sem, recv_sem, sib_send, sib_recv, mix_send, mix_recv, st_send, st_recv):
    width = points.shape[1]
    half = span // 2
    wide = width // 2
    scale2 = LOG2E / math.sqrt(width)
    row_index, col_index = lax.axis_index("row"), lax.axis_index("col")
    x_hi, y, core = row_index // 8, (row_index // 2) % 4, row_index % 2
    z, x_lo = col_index // 2, col_index % 2
    x = x_hi * 2 + x_lo

    def device(dx=0, dy=0, dz=0, flip=False):
        tx, ty, tz = (x + dx + 4) % 4, (y + dy + 4) % 4, (z + dz + 8) % 8
        tc = 1 - core if flip else core
        return ((tx // 2 * 4 + ty) * 2 + tc, tz * 2 + tx % 2)

    base = {}
    first = []
    total = 0
    for slots in STEPS:
        first.append(total)
        for plane in range(2):
            for slot in slots:
                base[slot, plane] = total
                total += span

    loads = []
    own_rows = pl.ds(pl.multiple_of(col_index * span, span), span)
    own = pltpu.make_async_copy(
        points.at[own_rows], keys.at[pl.ds(base[(0, 0), 0], span)], load_sem.at[0]
    )
    own.start()
    for place, dz in enumerate(ORDER):
        start = pl.multiple_of((((z + dz + 8) % 8) * 2 + x_lo) * span, span)
        load = pltpu.make_async_copy(
            points.at[pl.ds(start, span)], queries.at[pl.ds(place * span, span)], load_sem.at[1 + place]
        )
        load.start()
        loads.append(load)

    barrier = pltpu.get_barrier_semaphore()
    partners = [device(dx=dx, dy=dy) for dx, dy in DIRS.values()]
    partners += [device(dz=1), device(dz=-1), device(flip=True)]
    for partner in partners:
        pl.semaphore_signal(barrier, inc=1, device_id=partner, device_id_type=MESH)
    pl.semaphore_wait(barrier, len(partners))

    messages = {}

    def send(way, slot, part, cols=None):
        dx, dy = DIRS[way]
        target = (wrap(slot[0] - dx), wrap(slot[1] - dy))
        offset = 0 if part == "A" else half
        lanes = pl.ds(0, width) if cols is None else pl.ds(cols * wide, wide)
        number = sum(len(copies) for copies in messages.values())
        copy = pltpu.make_async_remote_copy(
            src_ref=keys.at[pl.ds(base[slot, 0] + offset, half), lanes],
            dst_ref=keys.at[pl.ds(base[target, 0] + offset, half), lanes],
            send_sem=send_sem.at[number],
            recv_sem=recv_sem.at[number],
            device_id=device(dx=dx, dy=dy),
            device_id_type=MESH,
        )
        copy.start()
        messages.setdefault((target, part), []).append(copy)

    def arrived(slot, part):
        for copy in messages[slot, part]:
            copy.wait_recv()

    siblings = {}

    def share(slot):
        number = len(siblings)
        copy = pltpu.make_async_remote_copy(
            src_ref=keys.at[pl.ds(base[slot, 0], span)],
            dst_ref=keys.at[pl.ds(base[slot, 1], span)],
            send_sem=sib_send.at[number],
            recv_sem=sib_recv.at[number],
            device_id=device(flip=True),
            device_id_type=MESH,
        )
        copy.start()
        siblings[slot] = copy

    def attend(step, start, rows, masked_from=None):
        count = 2 * len(STEPS[step]) * span
        mine = pl.ds(start, rows)
        block = keys[pl.ds(first[step], count), :]
        scores = lax.dot_general(
            queries[mine, :], block, (((1,), (1,)), ((), ())), preferred_element_type=jnp.float32
        ) * scale2
        if masked_from is not None:
            r = lax.broadcasted_iota(jnp.int32, scores.shape, 0) - masked_from
            c = lax.broadcasted_iota(jnp.int32, scores.shape, 1)
            scores = jnp.where(r == c, NEG, scores)
        top = jnp.max(scores, axis=1, keepdims=True)
        if step > 0:
            before = tops[mine, 0:1]
            top = jnp.maximum(top, before)
            shrink = jnp.exp2(before - top)
        weight = jnp.exp2(scores - top).astype(jnp.bfloat16)
        mass = jnp.sum(weight.astype(jnp.float32), axis=1, keepdims=True)
        mix = jnp.dot(weight, block, preferred_element_type=jnp.float32)
        if step > 0:
            mass = mass + sums[mine, 0:1] * shrink
            mix = mix + acc[mine, :] * shrink
        acc[mine, :] = mix
        tops[mine, :] = jnp.broadcast_to(top, (rows, 128))
        sums[mine, :] = jnp.broadcast_to(mass, (rows, 128))

    own.wait()
    for way in ("x+", "x-"):
        send(way, (0, 0), "A")
    for way in ("y+", "y-"):
        send(way, (0, 0), "B")
    for way in ("x+", "x-"):
        send(way, (0, 0), "B")
    for way in ("y+", "y-"):
        send(way, (0, 0), "A")
    share((0, 0))
    for load in loads:
        load.wait()

    arrived((-1, 0), "A")
    send("x+", (-1, 0), "A", 0)
    arrived((1, 0), "A")
    send("x-", (1, 0), "A", 1)
    arrived((0, -1), "B")
    send("y+", (0, -1), "B", 0)
    arrived((0, 1), "B")
    send("y-", (0, 1), "B", 1)
    for side in (1, -1):
        for way in ("y+", "y-"):
            send(way, (side, 0), "A")
        for way in ("x+", "x-"):
            send(way, (0, side), "B")
    arrived((-1, 0), "B")
    send("x+", (-1, 0), "B", 0)
    arrived((1, 0), "B")
    send("x-", (1, 0), "B", 1)
    arrived((0, -1), "A")
    send("y+", (0, -1), "A", 0)
    arrived((0, 1), "A")
    send("y-", (0, 1), "A", 1)
    for slot in STEPS[0][1:]:
        share(slot)
    for slot in STEPS[0]:
        siblings[slot].wait_recv()

    group = 2 * span
    last = (len(ORDER) - 1) * span
    attend(0, 0, group)
    attend(0, group, group)
    arrived((2, 0), "A")
    arrived((0, 2), "B")
    for way in ("y+", "y-"):
        send(way, (2, 0), "A")
    for way in ("x+", "x-"):
        send(way, (0, 2), "B")
    attend(0, 2 * group, group)
    attend(0, 3 * group, group, masked_from=span)

    for side in (1, -1):
        arrived((side, -1), "A")
        send("y+", (side, -1), "A", 0)
        arrived((side, 1), "A")
        send("y-", (side, 1), "A", 1)
        arrived((-1, side), "B")
        send("x+", (-1, side), "B", 0)
        arrived((1, side), "B")
        send("x-", (1, side), "B", 1)
    for slot in STEPS[1]:
        share(slot)
    for slot in STEPS[1]:
        siblings[slot].wait_recv()
    attend(1, 0, group)
    attend(1, group, group)

    arrived((2, 0), "B")
    arrived((0, 2), "A")
    for slot in STEPS[2]:
        share(slot)
    arrived((2, -1), "A")
    send("y+", (2, -1), "A", 0)
    arrived((2, 1), "A")
    send("y-", (2, 1), "A", 1)
    arrived((-1, 2), "B")
    send("x+", (-1, 2), "B", 0)
    arrived((1, 2), "B")
    send("x-", (1, 2), "B", 1)
    attend(1, 2 * group, group)
    attend(1, 3 * group, group)
    for slot in STEPS[2]:
        siblings[slot].wait_recv()
    for place in range(4):
        attend(2, place * group, group)
    for side in (1, -1):
        arrived((side, 2), "A")
        share((side, 2))
        arrived((2, side), "B")
        share((2, side))
    arrived((2, 2), "A")
    arrived((2, 2), "B")
    share((2, 2))
    for slot in STEPS[3]:
        siblings[slot].wait_recv()

    def note(place):
        mine = pl.ds(place * span, span)
        lane = lax.broadcasted_iota(jnp.int32, (span, 128), 1)
        pair = jnp.where(lane == 0, tops[mine, :], jnp.where(lane == 1, sums[mine, :], 0.0))
        pair = jnp.concatenate([pair, jnp.zeros((128 - span, 128), jnp.float32)], axis=0)
        own_stats[place] = jnp.transpose(pair)[0:8, :]

    hops = {}

    def start_hop(side, hop, part):
        sign = 1 - 2 * side
        number = (side * 4 + hop) * 2 + part
        if hop < 3:
            source, target = out_mix.at[(side * 3 + hop) * 2 + part], in_mix.at[(side * 3 + hop) * 2 + part]
        else:
            source, target = out_last.at[side * 2 + part], in_last.at[side * 2 + part]
        pair = []
        for src, dst, snd, rcv in (
            (out_stats.at[number], in_stats.at[number], st_send, st_recv),
            (source, target, mix_send, mix_recv),
        ):
            copy = pltpu.make_async_remote_copy(
                src_ref=src, dst_ref=dst, send_sem=snd.at[number], recv_sem=rcv.at[number],
                device_id=device(dz=sign), device_id_type=MESH,
            )
            copy.start()
            pair.append(copy)
        hops[side, hop, part] = pair

    def columns(factors):
        padded = jnp.concatenate([factors, jnp.zeros((128 - factors.shape[0], 128), jnp.float32)], axis=0)
        return jnp.transpose(padded)

    def incoming(side, hop, part):
        for copy in hops[side, hop, part]:
            copy.wait_recv()
        if hop < 3:
            values = in_mix[(side * 3 + hop) * 2 + part].astype(jnp.float32)
        else:
            values = in_last[side * 2 + part]
        stats = in_stats[(side * 4 + hop) * 2 + part]
        return values, stats

    def forward(side, hop, part, merge):
        place = ORDER.index(4 if hop == 0 else (1 - 2 * side) * (4 - hop))
        number = (side * 4 + hop) * 2 + part
        values = acc[pl.ds(place * span + part * half, half), :]
        stats = own_stats[place]
        if merge:
            other, other_stats = incoming(side, hop - 1, part)
            top = jnp.maximum(stats[0:1], other_stats[0:1])
            mine, theirs = jnp.exp2(stats[0:1] - top), jnp.exp2(other_stats[0:1] - top)
            mass = stats[1:2] * mine + other_stats[1:2] * theirs
            out_stats[number, 0:1, :] = top
            out_stats[number, 1:2, :] = mass
            factor = columns(jnp.concatenate([mine, theirs], axis=0))[part * half:(part + 1) * half]
            values = values * factor[:, 0:1] + other * factor[:, 1:2]
        else:
            out_stats[number] = stats
        if hop < 3:
            out_mix[(side * 3 + hop) * 2 + part] = values.astype(jnp.bfloat16)
        else:
            out_last[side * 2 + part] = values
        start_hop(side, hop, part)

    attend(3, 0, span)
    note(0)
    for side in (0, 1):
        forward(side, 0, side, False)
    for hop in (1, 2, 3):
        place = 2 * hop - 1
        attend(3, place * span, group)
        note(place)
        note(place + 1)
        for step in (0, 1):
            for side in (0, 1):
                part = 1 - side if step == 0 else side
                forward(side, hop, part, hop > 1 or part == side)
    attend(3, last, span)
    note(len(ORDER) - 1)

    stats = own_stats[len(ORDER) - 1]
    lane = lax.broadcasted_iota(jnp.int32, (1, 128), 1)
    answer = jnp.zeros((1, 128), jnp.float32)
    for step in (0, 1):
        for part in ((1, 0)[step],):
            plus, plus_stats = incoming(0, 3, part)
            minus, minus_stats = incoming(1, 3, part)
            top = jnp.maximum(stats[0:1], jnp.maximum(plus_stats[0:1], minus_stats[0:1]))
            f0 = jnp.exp2(stats[0:1] - top)
            f1 = jnp.exp2(plus_stats[0:1] - top)
            f2 = jnp.exp2(minus_stats[0:1] - top)
            mass = stats[1:2] * f0 + plus_stats[1:2] * f1 + minus_stats[1:2] * f2
            value = (top + jnp.log2(mass)) * LN2
            answer = jnp.where((lane >= part * half) & (lane < (part + 1) * half), value, answer)
            shares = jnp.concatenate([f0 / mass, f1 / mass, f2 / mass], axis=0)
            factor = columns(shares)[part * half:(part + 1) * half]
            values = acc[pl.ds(last + part * half, half), :] * factor[:, 0:1]
            values = values + plus * factor[:, 1:2] + minus * factor[:, 2:3]
            recon[pl.ds(part * half, half), :] = values
    density[...] = answer[:, :span]

    for copies in messages.values():
        for copy in copies:
            copy.wait_send()
    for copy in siblings.values():
        copy.wait_send()
    for pair in hops.values():
        for copy in pair:
            copy.wait_send()


def shards(points):
    span = points.shape[0] // lax.axis_size("col")
    width = points.shape[1]
    half = span // 2
    dma = pltpu.SemaphoreType.DMA
    vmem = pltpu.VMEM
    recon, density = pl.pallas_call(
        functools.partial(kernel, span),
        out_shape=(
            jax.ShapeDtypeStruct((span, width), jnp.float32),
            jax.ShapeDtypeStruct((1, span), jnp.float32),
        ),
        in_specs=[pl.BlockSpec(memory_space=pl.ANY)],
        out_specs=(pl.BlockSpec(memory_space=pltpu.VMEM), pl.BlockSpec(memory_space=pltpu.VMEM)),
        scratch_shapes=[
            vmem((32 * span, width), jnp.bfloat16),
            vmem((8 * span, width), jnp.bfloat16),
            vmem((8 * span, width), jnp.float32),
            vmem((8 * span, 128), jnp.float32),
            vmem((8 * span, 128), jnp.float32),
            vmem((8, 8, 128), jnp.float32),
            vmem((12, half, width), jnp.bfloat16),
            vmem((12, half, width), jnp.bfloat16),
            vmem((4, half, width), jnp.float32),
            vmem((4, half, width), jnp.float32),
            vmem((16, 8, 128), jnp.float32),
            vmem((16, 8, 128), jnp.float32),
            dma((9,)),
            dma((40,)),
            dma((40,)),
            dma((16,)),
            dma((16,)),
            dma((16,)),
            dma((16,)),
            dma((16,)),
            dma((16,)),
        ],
        compiler_params=pltpu.CompilerParams(
            collective_id=0, has_side_effects=True, vmem_limit_bytes=48 * 1024 * 1024
        ),
        cost_estimate=pl.CostEstimate(
            flops=4 * 8 * span * 32 * span * width,
            bytes_accessed=16 * span * width * 2,
            transcendentals=8 * span * 32 * span,
        ),
    )(points)
    return density.reshape(span), recon


def solution(mesh):
    return jax.shard_map(
        shards,
        mesh=mesh,
        in_specs=(P("row", None),),
        out_specs=(P(("row", "col")), P(("row", "col"), None)),
        check_vma=False,
    )
```

```python
import functools
import math

import jax
import jax.numpy as jnp
from jax import lax
from jax.experimental import pallas as pl
from jax.experimental.pallas import tpu as pltpu
from jax.sharding import PartitionSpec as P

MESH = pl.DeviceIdType.MESH
NEG = -1e30
LOG2E = math.log2(math.e)
LN2 = math.log(2.0)

NX, NY, NZ = 4, 4, 8
STEPS = (
    ((0, 0), (1, 0), (-1, 0), (0, 1), (0, -1)),
    ((1, 1), (1, -1), (-1, 1), (-1, -1)),
    ((2, 0), (0, 2)),
    ((1, 2), (-1, 2), (2, 1), (2, -1), (2, 2)),
)
PIECES = 2
SPREAD = 120.0
TINY = 1e-30
ORDER = (4, 3, -3, 2, -2, 1, -1, 0)
DIRS = {"x+": (1, 0), "x-": (-1, 0), "y+": (0, 1), "y-": (0, -1)}


def wrap(v):
    v %= 4
    return v - 4 if v == 3 else v


def kernel(span, points, recon, density, keys, queries, acc, tops, sums, own_stats,
           in_mix, out_mix, in_stats, out_stats,
           load_sem, send_sem, recv_sem, sib_send, sib_recv, mix_send, mix_recv, st_send, st_recv):
    width = points.shape[1]
    half = span // 2
    wide = width // 2
    scale2 = LOG2E / math.sqrt(width)
    row_index, col_index = lax.axis_index("row"), lax.axis_index("col")
    x_hi, y, core = row_index // 8, (row_index // 2) % 4, row_index % 2
    z, x_lo = col_index // 2, col_index % 2
    x = x_hi * 2 + x_lo

    def device(dx=0, dy=0, dz=0, flip=False):
        tx, ty, tz = (x + dx + 4) % 4, (y + dy + 4) % 4, (z + dz + 8) % 8
        tc = 1 - core if flip else core
        return ((tx // 2 * 4 + ty) * 2 + tc, tz * 2 + tx % 2)

    base = {}
    first = []
    total = 0
    for slots in STEPS:
        first.append(total)
        for plane in range(2):
            for slot in slots:
                base[slot, plane] = total
                total += span

    loads = []
    own_rows = pl.ds(pl.multiple_of(col_index * span, span), span)
    own = pltpu.make_async_copy(
        points.at[own_rows], keys.at[pl.ds(base[(0, 0), 0], span)], load_sem.at[0]
    )
    own.start()
    for place, dz in enumerate(ORDER):
        start = pl.multiple_of((((z + dz + 8) % 8) * 2 + x_lo) * span, span)
        load = pltpu.make_async_copy(
            points.at[pl.ds(start, span)], queries.at[pl.ds(place * span, span)], load_sem.at[1 + place]
        )
        load.start()
        loads.append(load)

    barrier = pltpu.get_barrier_semaphore()
    partners = [device(dx=dx, dy=dy) for dx, dy in DIRS.values()]
    partners += [device(dz=1), device(dz=-1), device(flip=True)]
    for partner in partners:
        pl.semaphore_signal(barrier, inc=1, device_id=partner, device_id_type=MESH)
    pl.semaphore_wait(barrier, len(partners))

    messages, seen = {}, set()

    def send(way, slot, part, cols=None):
        dx, dy = DIRS[way]
        target = (wrap(slot[0] - dx), wrap(slot[1] - dy))
        offset = 0 if part == "A" else half
        lanes = pl.ds(0, width) if cols is None else pl.ds(cols * wide, wide)
        number = sum(len(copies) for copies in messages.values())
        copy = pltpu.make_async_remote_copy(
            src_ref=keys.at[pl.ds(base[slot, 0] + offset, half), lanes],
            dst_ref=keys.at[pl.ds(base[target, 0] + offset, half), lanes],
            send_sem=send_sem.at[number],
            recv_sem=recv_sem.at[number],
            device_id=device(dx=dx, dy=dy),
            device_id_type=MESH,
        )
        copy.start()
        messages.setdefault((target, part), []).append(copy)

    def arrived(slot, part):
        if (slot, part) not in seen:
            seen.add((slot, part))
            for copy in messages[slot, part]:
                copy.wait_recv()

    siblings = {}

    def share(slot, part=None):
        number = len(siblings)
        rows = span if part is None else half
        offset = half if part == "B" else 0
        copy = pltpu.make_async_remote_copy(
            src_ref=keys.at[pl.ds(base[slot, 0] + offset, rows)],
            dst_ref=keys.at[pl.ds(base[slot, 1] + offset, rows)],
            send_sem=sib_send.at[number],
            recv_sem=sib_recv.at[number],
            device_id=device(flip=True),
            device_id_type=MESH,
        )
        copy.start()
        siblings[slot, part] = copy

    def attend(step, start, rows, masked_from=None):
        count = 2 * len(STEPS[step]) * span
        mine = pl.ds(start, rows)
        block = keys[pl.ds(first[step], count), :]
        scores = lax.dot_general(
            queries[mine, :], block, (((1,), (1,)), ((), ())), preferred_element_type=jnp.float32
        ) * scale2
        if masked_from is not None:
            r = lax.broadcasted_iota(jnp.int32, scores.shape, 0) - masked_from
            c = lax.broadcasted_iota(jnp.int32, scores.shape, 1)
            scores = jnp.where(r == c, NEG, scores)
        top = jnp.max(scores, axis=1, keepdims=True)
        if step > 0:
            before = tops[mine, 0:1]
            top = jnp.maximum(top, before)
            shrink = jnp.exp2(before - top)
        weight = jnp.exp2(scores - top).astype(jnp.bfloat16)
        mass = jnp.sum(weight.astype(jnp.float32), axis=1, keepdims=True)
        mix = jnp.dot(weight, block, preferred_element_type=jnp.float32)
        if step > 0:
            mass = mass + sums[mine, 0:1] * shrink
            mix = mix + acc[mine, :] * shrink
        acc[mine, :] = mix
        tops[mine, :] = jnp.broadcast_to(top, (rows, 128))
        sums[mine, :] = jnp.broadcast_to(mass, (rows, 128))

    own.wait()
    for way in ("x+", "x-"):
        send(way, (0, 0), "A")
    for way in ("y+", "y-"):
        send(way, (0, 0), "B")
    for way in ("x+", "x-"):
        send(way, (0, 0), "B")
    for way in ("y+", "y-"):
        send(way, (0, 0), "A")
    share((0, 0))
    for load in loads:
        load.wait()

    def pass_on(side_x, part_x, part_y):
        arrived((-1, side_x), part_x)
        send("x+", (-1, side_x), part_x, 0)
        arrived((1, side_x), part_x)
        send("x-", (1, side_x), part_x, 1)
        arrived((side_x, -1), part_y)
        send("y+", (side_x, -1), part_y, 0)
        arrived((side_x, 1), part_y)
        send("y-", (side_x, 1), part_y, 1)

    pass_on(0, "A", "B")
    for side in (1, -1):
        for way in ("y+", "y-"):
            send(way, (side, 0), "A")
        for way in ("x+", "x-"):
            send(way, (0, side), "B")
    for slot in STEPS[0][1:]:
        arrived(slot, "A")
        arrived(slot, "B")
        share(slot)
    arrived((2, 0), "A")
    arrived((0, 2), "B")
    for way in ("y+", "y-"):
        send(way, (2, 0), "A")
    for way in ("x+", "x-"):
        send(way, (0, 2), "B")
    pass_on(0, "B", "A")
    for slot in STEPS[0]:
        siblings[slot, None].wait_recv()

    most = 4 * span
    attend(0, 0, most)
    attend(0, most, most, masked_from=3 * span)

    for side in (1, -1):
        pass_on(side, "B", "A")
    for slot in STEPS[1]:
        share(slot)
    arrived((2, 0), "B")
    arrived((0, 2), "A")
    for slot in STEPS[2]:
        share(slot)
    for slot in STEPS[1]:
        siblings[slot, None].wait_recv()
    attend(1, 0, most)
    pass_on(2, "B", "A")
    for side in (1, -1):
        share((2, side), "A")
        share((side, 2), "B")
    attend(1, most, most)
    for slot in STEPS[2]:
        siblings[slot, None].wait_recv()
    attend(2, 0, most)
    attend(2, most, most)
    for side in (1, -1):
        arrived((side, 2), "A")
        share((side, 2), "A")
        arrived((2, side), "B")
        share((2, side), "B")
    for part in ("A", "B"):
        arrived((2, 2), part)
        share((2, 2), part)
    for slot in STEPS[3]:
        for part in ("A", "B"):
            siblings[slot, part].wait_recv()

    def note(place):
        mine = pl.ds(place * span, span)
        lane = lax.broadcasted_iota(jnp.int32, (span, 128), 1)
        pair = jnp.where(lane == 0, tops[mine, :], jnp.where(lane == 1, sums[mine, :], 0.0))
        pair = jnp.concatenate([pair, jnp.zeros((128 - span, 128), jnp.float32)], axis=0)
        own_stats[place] = jnp.transpose(pair)[0:8, :]

    hops, notes = {}, {}
    piece_width = width // PIECES

    def columns(factors):
        padded = jnp.concatenate([factors, jnp.zeros((128 - factors.shape[0], 128), jnp.float32)], axis=0)
        return jnp.transpose(padded)

    def start_note(side, hop, part):
        number = (side * 4 + hop) * 2 + part
        copy = pltpu.make_async_remote_copy(
            src_ref=out_stats.at[number], dst_ref=in_stats.at[number],
            send_sem=st_send.at[number], recv_sem=st_recv.at[number],
            device_id=device(dz=1 - 2 * side), device_id_type=MESH,
        )
        copy.start()
        notes[side, hop, part] = copy

    def start_piece(side, hop, part, piece):
        number = (side * 4 + hop) * 2 + part
        lanes = pl.ds(piece * piece_width, piece_width)
        copy = pltpu.make_async_remote_copy(
            src_ref=out_mix.at[number, :, lanes], dst_ref=in_mix.at[number, :, lanes],
            send_sem=mix_send.at[number * PIECES + piece], recv_sem=mix_recv.at[number * PIECES + piece],
            device_id=device(dz=1 - 2 * side), device_id_type=MESH,
        )
        copy.start()
        hops[side, hop, part, piece] = copy

    def forward(hop, parts, merge):
        place = [ORDER.index(4 if hop == 0 else (1 - 2 * side) * (4 - hop)) for side in (0, 1)]
        number = [(side * 4 + hop) * 2 + parts[side] for side in (0, 1)]
        factor = [None, None]
        for side in (0, 1):
            stats = own_stats[place[side]]
            if merge:
                notes[side, hop - 1, parts[side]].wait_recv()
                other = in_stats[number[side] - 2]
                top = jnp.maximum(stats[0:1], other[0:1])
                mine, theirs = jnp.exp2(stats[0:1] - top), jnp.exp2(other[0:1] - top)
                out_stats[number[side], 0:1, :] = top
                out_stats[number[side], 1:2, :] = stats[1:2] * mine + other[1:2] * theirs
                first = parts[side] * half
                factor[side] = columns(jnp.concatenate([mine, theirs], axis=0))[first:first + half]
            else:
                out_stats[number[side]] = stats
            if hop < 3:
                start_note(side, hop, parts[side])
        peaks = [jnp.zeros((half, 128), jnp.float32)] * 2
        for piece in range(PIECES):
            lanes = pl.ds(piece * piece_width, piece_width)
            for side in (0, 1):
                values = acc[pl.ds(place[side] * span + parts[side] * half, half), lanes]
                if merge:
                    hops[side, hop - 1, parts[side], piece].wait_recv()
                    other = in_mix[number[side] - 2, :, lanes].astype(jnp.float32)
                    values = values * factor[side][:, 0:1] + other * factor[side][:, 1:2]
                if hop == 3:
                    peak = jnp.maximum(jnp.max(jnp.abs(values), axis=1, keepdims=True), TINY)
                    lane = lax.broadcasted_iota(jnp.int32, (half, 128), 1)
                    peaks[side] = jnp.where(lane == piece, peak, peaks[side])
                    values = jnp.exp2(values * (SPREAD / peak))
                out_mix[number[side], :, lanes] = values.astype(jnp.bfloat16)
                start_piece(side, hop, parts[side], piece)
        if hop == 3:
            for side in (0, 1):
                rows = [peaks[side], jnp.zeros((128 - (parts[side] + 1) * half, 128), jnp.float32)]
                if parts[side]:
                    rows.insert(0, jnp.zeros((parts[side] * half, 128), jnp.float32))
                rows = jnp.transpose(jnp.concatenate(rows, axis=0))
                out_stats[number[side], 2:2 + PIECES, :] = rows[0:PIECES]
                start_note(side, hop, parts[side])

    attend(3, 0, most)
    note(0)
    forward(0, (0, 1), False)
    note(1)
    note(2)
    forward(1, (1, 0), False)
    note(3)
    attend(3, most, most)
    forward(1, (0, 1), True)
    for place in range(4, 8):
        note(place)
    for hop in (2, 3):
        forward(hop, (1, 0), True)
        forward(hop, (0, 1), True)

    last = 7 * span
    stats = own_stats[7]
    lane = lax.broadcasted_iota(jnp.int32, (1, 128), 1)
    answer = jnp.zeros((1, 128), jnp.float32)
    for part in (0, 1):
        for side in (0, 1):
            notes[side, 3, part].wait_recv()
        plus, minus = in_stats[6 + part], in_stats[14 + part]
        top = jnp.maximum(stats[0:1], jnp.maximum(plus[0:1], minus[0:1]))
        f0 = jnp.exp2(stats[0:1] - top)
        f1 = jnp.exp2(plus[0:1] - top)
        f2 = jnp.exp2(minus[0:1] - top)
        mass = stats[1:2] * f0 + plus[1:2] * f1 + minus[1:2] * f2
        value = (top + jnp.log2(mass)) * LN2
        answer = jnp.where((lane >= part * half) & (lane < (part + 1) * half), value, answer)
        shares = [f0 / mass]
        for f, got in ((f1, plus), (f2, minus)):
            shares.append(got[2:2 + PIECES] * (f / (mass * SPREAD)))
        factor = columns(jnp.concatenate(shares, axis=0))[part * half:(part + 1) * half]
        for piece in range(PIECES):
            lanes = pl.ds(piece * piece_width, piece_width)
            values = acc[pl.ds(last + part * half, half), lanes] * factor[:, 0:1]
            for side in (0, 1):
                hops[side, 3, part, piece].wait_recv()
                sent = jnp.log2(in_mix[side * 8 + 6 + part, :, lanes].astype(jnp.float32))
                at = 1 + side * PIECES + piece
                values = values + sent * factor[:, at:at + 1]
            recon[pl.ds(part * half, half), lanes] = values
    density[...] = answer[:, :span]

    for copies in messages.values():
        for copy in copies:
            copy.wait_send()
    for group in (siblings, hops, notes):
        for copy in group.values():
            copy.wait_send()


def shards(points):
    span = points.shape[0] // lax.axis_size("col")
    width = points.shape[1]
    half = span // 2
    dma = pltpu.SemaphoreType.DMA
    vmem = pltpu.VMEM
    recon, density = pl.pallas_call(
        functools.partial(kernel, span),
        out_shape=(
            jax.ShapeDtypeStruct((span, width), jnp.float32),
            jax.ShapeDtypeStruct((1, span), jnp.float32),
        ),
        in_specs=[pl.BlockSpec(memory_space=pltpu.HBM)],
        out_specs=(pl.BlockSpec(memory_space=pltpu.VMEM), pl.BlockSpec(memory_space=pltpu.VMEM)),
        scratch_shapes=[
            vmem((32 * span, width), jnp.bfloat16),
            vmem((8 * span, width), jnp.bfloat16),
            vmem((8 * span, width), jnp.float32),
            vmem((8 * span, 128), jnp.float32),
            vmem((8 * span, 128), jnp.float32),
            vmem((8, 8, 128), jnp.float32),
            vmem((16, half, width), jnp.bfloat16),
            vmem((16, half, width), jnp.bfloat16),
            vmem((16, 8, 128), jnp.float32),
            vmem((16, 8, 128), jnp.float32),
            dma((9,)),
            dma((40,)),
            dma((40,)),
            dma((21,)),
            dma((21,)),
            dma((16 * PIECES,)),
            dma((16 * PIECES,)),
            dma((16,)),
            dma((16,)),
        ],
        compiler_params=pltpu.CompilerParams(
            collective_id=0, has_side_effects=True, vmem_limit_bytes=62 * 1024 * 1024
        ),
        cost_estimate=pl.CostEstimate(
            flops=4 * 8 * span * 32 * span * width,
            bytes_accessed=16 * span * width * 2,
            transcendentals=8 * span * 32 * span,
        ),
    )(points)
    return density.reshape(span), recon


def solution(mesh):
    return jax.shard_map(
        shards,
        mesh=mesh,
        in_specs=(P("row", None),),
        out_specs=(P(("row", "col")), P(("row", "col"), None)),
        check_vma=False,
    )
```

```python
import functools
import math

import jax
import jax.numpy as jnp
from jax import lax
from jax.experimental import pallas as pl
from jax.experimental.pallas import tpu as pltpu
from jax.sharding import PartitionSpec as P

MESH = pl.DeviceIdType.MESH
NEG = -1e30
LOG2E = math.log2(math.e)
LN2 = math.log(2.0)

NX, NY, NZ = 4, 4, 8
STEPS = (
    ((0, 0), (1, 0), (-1, 0), (0, 1), (0, -1)),
    ((1, 1), (1, -1), (-1, 1), (-1, -1)),
    ((2, 0), (0, 2)),
    ((1, 2), (-1, 2), (2, 1), (2, -1), (2, 2)),
)
PIECES = 2
SPREAD = 120.0
TINY = 1e-30
ORDER = (4, 3, -3, 2, -2, 1, -1, 0)
DIRS = {"x+": (1, 0), "x-": (-1, 0), "y+": (0, 1), "y-": (0, -1)}


def wrap(v):
    v %= 4
    return v - 4 if v == 3 else v


def kernel(span, points, recon, density, keys, queries, acc, tops, sums, peaks, own_stats,
           in_mix, out_mix, in_stats, out_stats,
           load_sem, send_sem, recv_sem, sib_send, sib_recv, mix_send, mix_recv, st_send, st_recv):
    width = points.shape[1]
    half = span // 2
    wide = width // 2
    scale2 = LOG2E / math.sqrt(width)
    row_index, col_index = lax.axis_index("row"), lax.axis_index("col")
    x_hi, y, core = row_index // 8, (row_index // 2) % 4, row_index % 2
    z, x_lo = col_index // 2, col_index % 2
    x = x_hi * 2 + x_lo

    def device(dx=0, dy=0, dz=0, flip=False):
        tx, ty, tz = (x + dx + 4) % 4, (y + dy + 4) % 4, (z + dz + 8) % 8
        tc = 1 - core if flip else core
        return ((tx // 2 * 4 + ty) * 2 + tc, tz * 2 + tx % 2)

    base = {}
    first = []
    total = 0
    for slots in STEPS:
        first.append(total)
        for plane in range(2):
            for slot in slots:
                base[slot, plane] = total
                total += span

    loads = []
    own_rows = pl.ds(pl.multiple_of(col_index * span, span), span)
    own = pltpu.make_async_copy(
        points.at[own_rows], keys.at[pl.ds(base[(0, 0), 0], span)], load_sem.at[0]
    )
    own.start()
    for place, dz in enumerate(ORDER):
        start = pl.multiple_of((((z + dz + 8) % 8) * 2 + x_lo) * span, span)
        load = pltpu.make_async_copy(
            points.at[pl.ds(start, span)], queries.at[pl.ds(place * span, span)], load_sem.at[1 + place]
        )
        load.start()
        loads.append(load)

    barrier = pltpu.get_barrier_semaphore()
    partners = [device(dx=dx, dy=dy) for dx, dy in DIRS.values()]
    partners += [device(dx=dx, dy=dy, flip=True) for dx, dy in DIRS.values()]
    partners += [device(dz=1), device(dz=-1), device(flip=True)]
    for partner in partners:
        pl.semaphore_signal(barrier, inc=1, device_id=partner, device_id_type=MESH)
    pl.semaphore_wait(barrier, len(partners))

    messages, waited, copies = {}, set(), []

    def send(way, slot, part, cols=None, plane=0):
        dx, dy = DIRS[way]
        target = (wrap(slot[0] - dx), wrap(slot[1] - dy))
        offset = 0 if part == "A" else half
        lanes = pl.ds(0, width) if cols is None else pl.ds(cols * wide, wide)
        copy = pltpu.make_async_remote_copy(
            src_ref=keys.at[pl.ds(base[slot, 0] + offset, half), lanes],
            dst_ref=keys.at[pl.ds(base[target, plane] + offset, half), lanes],
            send_sem=send_sem.at[len(copies)],
            recv_sem=recv_sem.at[len(copies)],
            device_id=device(dx=dx, dy=dy, flip=plane == 1),
            device_id_type=MESH,
        )
        copy.start()
        messages.setdefault((target, part, plane), []).append((cols, len(copies)))
        copies.append(copy)

    def send_halves(way, slot, part):
        for cols in ((0, 1) if way in ("x+", "y+") else (1, 0)):
            send(way, slot, part, cols)

    def arrived(slot, part, cols=None, plane=0):
        for held, number in messages[slot, part, plane]:
            if number not in waited and (cols is None or held is None or held == cols):
                waited.add(number)
                copies[number].wait_recv()

    siblings = {}

    def share(slot, part=None):
        number = len(siblings)
        rows = span if part is None else half
        offset = half if part == "B" else 0
        copy = pltpu.make_async_remote_copy(
            src_ref=keys.at[pl.ds(base[slot, 0] + offset, rows)],
            dst_ref=keys.at[pl.ds(base[slot, 1] + offset, rows)],
            send_sem=sib_send.at[number],
            recv_sem=sib_recv.at[number],
            device_id=device(flip=True),
            device_id_type=MESH,
        )
        copy.start()
        siblings[slot, part] = copy

    def attend(step, start, rows, masked_from=None):
        count = 2 * len(STEPS[step]) * span
        mine = pl.ds(start, rows)
        block = keys[pl.ds(first[step], count), :]
        scores = lax.dot_general(
            queries[mine, :], block, (((1,), (1,)), ((), ())), preferred_element_type=jnp.float32
        ) * scale2
        if masked_from is not None:
            r = lax.broadcasted_iota(jnp.int32, scores.shape, 0) - masked_from
            c = lax.broadcasted_iota(jnp.int32, scores.shape, 1)
            scores = jnp.where(r == c, NEG, scores)
        top = jnp.max(scores, axis=1, keepdims=True)
        if step > 0:
            before = tops[mine, 0:1]
            top = jnp.maximum(top, before)
            shrink = jnp.exp2(before - top)
        weight = jnp.exp2(scores - top).astype(jnp.bfloat16)
        mass = jnp.sum(weight.astype(jnp.float32), axis=1, keepdims=True)
        mix = jnp.dot(weight, block, preferred_element_type=jnp.float32)
        if step > 0:
            mass = mass + sums[mine, 0:1] * shrink
            mix = mix + acc[mine, :] * shrink
        acc[mine, :] = mix
        tops[mine, :] = jnp.broadcast_to(top, (rows, 128))
        sums[mine, :] = jnp.broadcast_to(mass, (rows, 128))

    own.wait()
    for way in ("x+", "x-"):
        send_halves(way, (0, 0), "A")
    for way in ("y+", "y-"):
        send_halves(way, (0, 0), "B")
    for way in ("x+", "x-"):
        send(way, (0, 0), "B")
    for way in ("y+", "y-"):
        send(way, (0, 0), "A")
    share((0, 0))
    for load in loads:
        load.wait()

    def pass_on(side, part_x, part_y, planes=(0,)):
        for way, slot, part, cols in (
            ("x+", (-1, side), part_x, 0), ("x-", (1, side), part_x, 1),
            ("y+", (side, -1), part_y, 0), ("y-", (side, 1), part_y, 1),
        ):
            arrived(slot, part, cols)
            for plane in planes:
                send(way, slot, part, cols, plane)

    pass_on(0, "A", "B")
    for side in (1, -1):
        arrived((side, 0), "A")
        for way in ("y+", "y-"):
            send(way, (side, 0), "A")
        arrived((0, side), "B")
        for way in ("x+", "x-"):
            send(way, (0, side), "B")
    for slot in STEPS[0][1:]:
        arrived(slot, "A")
        arrived(slot, "B")
        share(slot)
    arrived((2, 0), "A")
    for way in ("y+", "y-"):
        send_halves(way, (2, 0), "A")
    arrived((0, 2), "B")
    for way in ("x+", "x-"):
        send_halves(way, (0, 2), "B")
    pass_on(0, "B", "A")
    for slot in STEPS[0]:
        siblings[slot, None].wait_recv()

    most = 4 * span
    attend(0, 0, most)
    pass_on(1, "B", "A")
    attend(0, most, most, masked_from=3 * span)
    pass_on(-1, "B", "A")
    for slot in STEPS[1]:
        arrived(slot, "A")
        arrived(slot, "B")
        share(slot)
    pass_on(2, "B", "A", (0, 1))
    for slot in STEPS[1]:
        siblings[slot, None].wait_recv()
    attend(1, 0, most)
    for slot in STEPS[2]:
        arrived(slot, "A")
        arrived(slot, "B")
        share(slot)
    for side in (1, -1):
        arrived((2, side), "A")
        share((2, side), "A")
        arrived((side, 2), "B")
        share((side, 2), "B")
    attend(1, most, most)
    for slot in STEPS[2]:
        siblings[slot, None].wait_recv()
    for side in (1, -1):
        arrived((side, 2), "A")
        share((side, 2), "A")
        arrived((2, side), "B")
        share((2, side), "B")
    attend(2, 0, most)
    attend(2, most, most)
    for part in ("A", "B"):
        for plane in (0, 1):
            arrived((2, 2), part, plane=plane)
    for slot in STEPS[3][:4]:
        for part in ("A", "B"):
            siblings[slot, part].wait_recv()

    def note(places):
        lane = lax.broadcasted_iota(jnp.int32, (span, 128), 1)
        table = jnp.zeros((span, 128), jnp.float32)
        for index, place in enumerate(places):
            mine = pl.ds(place * span, span)
            peak = jnp.maximum(jnp.max(jnp.abs(acc[mine, :]), axis=1, keepdims=True), TINY)
            peaks[mine, :] = jnp.broadcast_to(peak, (span, 128))
            for row, values in enumerate((tops[mine, :], sums[mine, :], peak)):
                table = jnp.where(lane == 3 * index + row, values, table)
        table = jnp.transpose(jnp.concatenate([table, jnp.zeros((128 - span, 128), jnp.float32)], axis=0))
        for index, place in enumerate(places):
            own_stats[place, 0:3, :] = table[3 * index:3 * index + 3]

    hops, notes = {}, {}
    piece_width = width // PIECES

    def columns(factors):
        padded = jnp.concatenate([factors, jnp.zeros((128 - factors.shape[0], 128), jnp.float32)], axis=0)
        return jnp.transpose(padded)

    def start_note(side, hop, part):
        number = (side * 4 + hop) * 2 + part
        copy = pltpu.make_async_remote_copy(
            src_ref=out_stats.at[number], dst_ref=in_stats.at[number],
            send_sem=st_send.at[number], recv_sem=st_recv.at[number],
            device_id=device(dz=1 - 2 * side), device_id_type=MESH,
        )
        copy.start()
        notes[side, hop, part] = copy

    def start_piece(side, hop, part, piece):
        number = (side * 4 + hop) * 2 + part
        lanes = pl.ds(piece * piece_width, piece_width)
        copy = pltpu.make_async_remote_copy(
            src_ref=out_mix.at[number, :, lanes], dst_ref=in_mix.at[number, :, lanes],
            send_sem=mix_send.at[number * PIECES + piece], recv_sem=mix_recv.at[number * PIECES + piece],
            device_id=device(dz=1 - 2 * side), device_id_type=MESH,
        )
        copy.start()
        hops[side, hop, part, piece] = copy

    def forward(hop, parts, merge):
        place = [ORDER.index(4 if hop == 0 else (1 - 2 * side) * (4 - hop)) for side in (0, 1)]
        number = [(side * 4 + hop) * 2 + parts[side] for side in (0, 1)]
        factor = [None, None]
        for side in (0, 1):
            first = parts[side] * half
            stats = own_stats[place[side]]
            if merge:
                notes[side, hop - 1, parts[side]].wait_recv()
                other = in_stats[number[side] - 2]
                top = jnp.maximum(stats[0:1], other[0:1])
                mine, theirs = jnp.exp2(stats[0:1] - top), jnp.exp2(other[0:1] - top)
                peak = stats[2:3] * mine + other[2:3] * theirs
                out_stats[number[side], 0:1, :] = top
                out_stats[number[side], 1:2, :] = stats[1:2] * mine + other[1:2] * theirs
                out_stats[number[side], 2:3, :] = peak
                start_note(side, hop, parts[side])
                shares = [mine * (SPREAD / peak), theirs * (other[2:3] / peak)]
                factor[side] = columns(jnp.concatenate(shares, axis=0))[first:first + half]
            else:
                out_stats[number[side]] = stats
                start_note(side, hop, parts[side])
                factor[side] = SPREAD / peaks[pl.ds(place[side] * span + first, half), :]
        for piece in range(PIECES):
            lanes = pl.ds(piece * piece_width, piece_width)
            for side in (0, 1):
                values = acc[pl.ds(place[side] * span + parts[side] * half, half), lanes] * factor[side][:, 0:1]
                if merge:
                    hops[side, hop - 1, parts[side], piece].wait_recv()
                    other = jnp.log2(in_mix[number[side] - 2, :, lanes].astype(jnp.float32))
                    values = values + other * factor[side][:, 1:2]
                out_mix[number[side], :, lanes] = jnp.exp2(values).astype(jnp.bfloat16)
                start_piece(side, hop, parts[side], piece)

    early = 3 * span
    attend(3, 0, early)
    note((0, 1, 2))
    forward(0, (0, 1), False)
    forward(1, (1, 0), False)
    attend(3, early, 5 * span)
    note((3, 4, 5, 6, 7))
    forward(1, (0, 1), True)
    for hop in (2, 3):
        forward(hop, (1, 0), True)
        forward(hop, (0, 1), True)

    last = 7 * span
    stats = own_stats[7]
    lane = lax.broadcasted_iota(jnp.int32, (1, 128), 1)
    answer = jnp.zeros((1, 128), jnp.float32)
    for part in (0, 1):
        for side in (0, 1):
            notes[side, 3, part].wait_recv()
        plus, minus = in_stats[6 + part], in_stats[14 + part]
        top = jnp.maximum(stats[0:1], jnp.maximum(plus[0:1], minus[0:1]))
        f0 = jnp.exp2(stats[0:1] - top)
        f1 = jnp.exp2(plus[0:1] - top)
        f2 = jnp.exp2(minus[0:1] - top)
        mass = stats[1:2] * f0 + plus[1:2] * f1 + minus[1:2] * f2
        value = (top + jnp.log2(mass)) * LN2
        answer = jnp.where((lane >= part * half) & (lane < (part + 1) * half), value, answer)
        shares = [f0 / mass, f1 * plus[2:3] / (mass * SPREAD), f2 * minus[2:3] / (mass * SPREAD)]
        factor = columns(jnp.concatenate(shares, axis=0))[part * half:(part + 1) * half]
        for piece in range(PIECES):
            lanes = pl.ds(piece * piece_width, piece_width)
            values = acc[pl.ds(last + part * half, half), lanes] * factor[:, 0:1]
            for side in (0, 1):
                hops[side, 3, part, piece].wait_recv()
                sent = jnp.log2(in_mix[side * 8 + 6 + part, :, lanes].astype(jnp.float32))
                values = values + sent * factor[:, 1 + side:2 + side]
            recon[pl.ds(part * half, half), lanes] = values
    density[...] = answer[:, :span]

    for copy in copies:
        copy.wait_send()
    for group in (siblings, hops, notes):
        for copy in group.values():
            copy.wait_send()


def shards(points):
    span = points.shape[0] // lax.axis_size("col")
    width = points.shape[1]
    half = span // 2
    dma = pltpu.SemaphoreType.DMA
    vmem = pltpu.VMEM
    recon, density = pl.pallas_call(
        functools.partial(kernel, span),
        out_shape=(
            jax.ShapeDtypeStruct((span, width), jnp.float32),
            jax.ShapeDtypeStruct((1, span), jnp.float32),
        ),
        in_specs=[pl.BlockSpec(memory_space=pltpu.HBM)],
        out_specs=(pl.BlockSpec(memory_space=pltpu.VMEM), pl.BlockSpec(memory_space=pltpu.VMEM)),
        scratch_shapes=[
            vmem((32 * span, width), jnp.bfloat16),
            vmem((8 * span, width), jnp.bfloat16),
            vmem((8 * span, width), jnp.float32),
            vmem((8 * span, 128), jnp.float32),
            vmem((8 * span, 128), jnp.float32),
            vmem((8 * span, 128), jnp.float32),
            vmem((8, 8, 128), jnp.float32),
            vmem((16, half, width), jnp.bfloat16),
            vmem((16, half, width), jnp.bfloat16),
            vmem((16, 8, 128), jnp.float32),
            vmem((16, 8, 128), jnp.float32),
            dma((9,)),
            dma((52,)),
            dma((52,)),
            dma((19,)),
            dma((19,)),
            dma((16 * PIECES,)),
            dma((16 * PIECES,)),
            dma((16,)),
            dma((16,)),
        ],
        compiler_params=pltpu.CompilerParams(
            collective_id=0, has_side_effects=True, vmem_limit_bytes=62 * 1024 * 1024
        ),
        cost_estimate=pl.CostEstimate(
            flops=4 * 8 * span * 32 * span * width,
            bytes_accessed=16 * span * width * 2,
            transcendentals=8 * span * 32 * span,
        ),
    )(points)
    return density.reshape(span), recon


def solution(mesh):
    return jax.shard_map(
        shards,
        mesh=mesh,
        in_specs=(P("row", None),),
        out_specs=(P(("row", "col")), P(("row", "col"), None)),
        check_vma=False,
    )
```

```python
import functools
import math

import jax
import jax.numpy as jnp
from jax import lax
from jax.experimental import pallas as pl
from jax.experimental.pallas import tpu as pltpu
from jax.sharding import PartitionSpec as P

MESH = pl.DeviceIdType.MESH
NEG = -1e30
LOG2E = math.log2(math.e)
LN2 = math.log(2.0)

NX, NY, NZ = 4, 4, 8
STEPS = (
    ((0, 0), (1, 0), (-1, 0), (0, 1), (0, -1)),
    ((1, 1), (1, -1), (-1, 1), (-1, -1), (2, 0), (0, 2)),
    ((1, 2), (-1, 2), (2, 1), (2, -1), (2, 2)),
)
PIECES = 2
SPREAD = 120.0
TINY = 1e-30
ORDER = (4, 3, -3, 2, -2, 1, -1, 0)
DIRS = {"x+": (1, 0), "x-": (-1, 0), "y+": (0, 1), "y-": (0, -1)}


def wrap(v):
    v %= 4
    return v - 4 if v == 3 else v


def kernel(span, points, recon, density, keys, queries, acc, tops, sums, peaks, own_stats,
           in_mix, out_mix, in_stats, out_stats,
           load_sem, send_sem, recv_sem, sib_send, sib_recv, mix_send, mix_recv, st_send, st_recv):
    width = points.shape[1]
    half = span // 2
    wide = width // 2
    scale2 = LOG2E / math.sqrt(width)
    row_index, col_index = lax.axis_index("row"), lax.axis_index("col")
    x_hi, y, core = row_index // 8, (row_index // 2) % 4, row_index % 2
    z, x_lo = col_index // 2, col_index % 2
    x = x_hi * 2 + x_lo

    def device(dx=0, dy=0, dz=0, flip=False):
        tx, ty, tz = (x + dx + 4) % 4, (y + dy + 4) % 4, (z + dz + 8) % 8
        tc = 1 - core if flip else core
        return ((tx // 2 * 4 + ty) * 2 + tc, tz * 2 + tx % 2)

    base = {}
    first = []
    total = 0
    for slots in STEPS:
        first.append(total)
        for plane in range(2):
            for slot in slots:
                base[slot, plane] = total
                total += span

    loads = []
    own_rows = pl.ds(pl.multiple_of(col_index * span, span), span)
    own = pltpu.make_async_copy(
        points.at[own_rows], keys.at[pl.ds(base[(0, 0), 0], span)], load_sem.at[0]
    )
    own.start()
    for place, dz in enumerate(ORDER):
        start = pl.multiple_of((((z + dz + 8) % 8) * 2 + x_lo) * span, span)
        load = pltpu.make_async_copy(
            points.at[pl.ds(start, span)], queries.at[pl.ds(place * span, span)], load_sem.at[1 + place]
        )
        load.start()
        loads.append(load)

    barrier = pltpu.get_barrier_semaphore()
    partners = [device(dx=dx, dy=dy) for dx, dy in DIRS.values()]
    partners += [device(dx=dx, dy=dy, flip=True) for dx, dy in DIRS.values()]
    partners += [device(dz=1), device(dz=-1), device(flip=True)]
    for partner in partners:
        pl.semaphore_signal(barrier, inc=1, device_id=partner, device_id_type=MESH)
    pl.semaphore_wait(barrier, len(partners))

    messages, waited, copies = {}, set(), []

    def send(way, slot, part, cols=None, plane=0):
        dx, dy = DIRS[way]
        target = (wrap(slot[0] - dx), wrap(slot[1] - dy))
        offset = 0 if part == "A" else half
        lanes = pl.ds(0, width) if cols is None else pl.ds(cols * wide, wide)
        copy = pltpu.make_async_remote_copy(
            src_ref=keys.at[pl.ds(base[slot, 0] + offset, half), lanes],
            dst_ref=keys.at[pl.ds(base[target, plane] + offset, half), lanes],
            send_sem=send_sem.at[len(copies)],
            recv_sem=recv_sem.at[len(copies)],
            device_id=device(dx=dx, dy=dy, flip=plane == 1),
            device_id_type=MESH,
        )
        copy.start()
        messages.setdefault((target, part, plane), []).append((cols, len(copies)))
        copies.append(copy)

    def send_halves(way, slot, part):
        for cols in ((0, 1) if way in ("x+", "y+") else (1, 0)):
            send(way, slot, part, cols)

    def arrived(slot, part, cols=None, plane=0):
        for held, number in messages[slot, part, plane]:
            if number not in waited and (cols is None or held is None or held == cols):
                waited.add(number)
                copies[number].wait_recv()

    siblings = {}

    def share(slot, part=None):
        number = len(siblings)
        rows = span if part is None else half
        offset = half if part == "B" else 0
        copy = pltpu.make_async_remote_copy(
            src_ref=keys.at[pl.ds(base[slot, 0] + offset, rows)],
            dst_ref=keys.at[pl.ds(base[slot, 1] + offset, rows)],
            send_sem=sib_send.at[number],
            recv_sem=sib_recv.at[number],
            device_id=device(flip=True),
            device_id_type=MESH,
        )
        copy.start()
        siblings[slot, part] = copy

    def score(step, start, rows):
        block = keys[pl.ds(first[step], 2 * len(STEPS[step]) * span), :]
        return lax.dot_general(
            queries[pl.ds(start, rows), :], block, (((1,), (1,)), ((), ())),
            preferred_element_type=jnp.float32,
        )

    def absorb(scores, step, start, rows, masked_from=None):
        mine = pl.ds(start, rows)
        block = keys[pl.ds(first[step], 2 * len(STEPS[step]) * span), :]
        scores = scores * scale2
        if masked_from is not None:
            r = lax.broadcasted_iota(jnp.int32, scores.shape, 0) - masked_from
            c = lax.broadcasted_iota(jnp.int32, scores.shape, 1)
            scores = jnp.where(r == c, NEG, scores)
        top = jnp.max(scores, axis=1, keepdims=True)
        if step > 0:
            before = tops[mine, 0:1]
            top = jnp.maximum(top, before)
            shrink = jnp.exp2(before - top)
        weight = jnp.exp2(scores - top).astype(jnp.bfloat16)
        mass = jnp.sum(weight.astype(jnp.float32), axis=1, keepdims=True)
        mix = jnp.dot(weight, block, preferred_element_type=jnp.float32)
        if step > 0:
            mass = mass + sums[mine, 0:1] * shrink
            mix = mix + acc[mine, :] * shrink
        acc[mine, :] = mix
        tops[mine, :] = jnp.broadcast_to(top, (rows, 128))
        sums[mine, :] = jnp.broadcast_to(mass, (rows, 128))

    own.wait()
    for way in ("x+", "x-"):
        send_halves(way, (0, 0), "A")
    for way in ("y+", "y-"):
        send_halves(way, (0, 0), "B")
    for way in ("x+", "x-"):
        send(way, (0, 0), "B")
    for way in ("y+", "y-"):
        send(way, (0, 0), "A")
    share((0, 0))
    for load in loads:
        load.wait()

    def pass_on(side, part_x, part_y, planes=(0,)):
        for way, slot, part, cols in (
            ("x+", (-1, side), part_x, 0), ("x-", (1, side), part_x, 1),
            ("y+", (side, -1), part_y, 0), ("y-", (side, 1), part_y, 1),
        ):
            arrived(slot, part, cols)
            for plane in planes:
                send(way, slot, part, cols, plane)

    pass_on(0, "A", "B")
    for side in (1, -1):
        arrived((side, 0), "A")
        for way in ("y+", "y-"):
            send(way, (side, 0), "A")
        arrived((0, side), "B")
        for way in ("x+", "x-"):
            send(way, (0, side), "B")
    for slot in STEPS[0][1:]:
        arrived(slot, "A")
        arrived(slot, "B")
        share(slot)
    arrived((2, 0), "A")
    for way in ("y+", "y-"):
        send_halves(way, (2, 0), "A")
    arrived((0, 2), "B")
    for way in ("x+", "x-"):
        send_halves(way, (0, 2), "B")
    pass_on(0, "B", "A")
    for slot in STEPS[0]:
        siblings[slot, None].wait_recv()

    most = 4 * span
    near, far = score(0, 0, most), score(0, most, most)
    absorb(near, 0, 0, most)
    pass_on(1, "B", "A")
    absorb(far, 0, most, most, masked_from=3 * span)
    pass_on(-1, "B", "A")
    for slot in STEPS[1][:4]:
        arrived(slot, "A")
        arrived(slot, "B")
        share(slot)
    pass_on(2, "B", "A", (0, 1))
    for slot in STEPS[1][4:]:
        arrived(slot, "A")
        arrived(slot, "B")
        share(slot)
    for slot in STEPS[1]:
        siblings[slot, None].wait_recv()
    near, far = score(1, 0, most), score(1, most, most)
    absorb(near, 1, 0, most)
    for side in (1, -1):
        for part in ("A", "B"):
            arrived((2, side), part)
            share((2, side), part)
            arrived((side, 2), part)
            share((side, 2), part)
    absorb(far, 1, most, most)
    for part in ("A", "B"):
        for plane in (0, 1):
            arrived((2, 2), part, plane=plane)
    for slot in STEPS[2][:4]:
        for part in ("A", "B"):
            siblings[slot, part].wait_recv()

    def note(places):
        lane = lax.broadcasted_iota(jnp.int32, (span, 128), 1)
        table = jnp.zeros((span, 128), jnp.float32)
        for index, place in enumerate(places):
            mine = pl.ds(place * span, span)
            peak = jnp.maximum(jnp.max(jnp.abs(acc[mine, :]), axis=1, keepdims=True), TINY)
            peaks[mine, :] = jnp.broadcast_to(peak, (span, 128))
            for row, values in enumerate((tops[mine, :], sums[mine, :], peak)):
                table = jnp.where(lane == 3 * index + row, values, table)
        table = jnp.transpose(jnp.concatenate([table, jnp.zeros((128 - span, 128), jnp.float32)], axis=0))
        for index, place in enumerate(places):
            own_stats[place, 0:3, :] = table[3 * index:3 * index + 3]

    hops, notes = {}, {}
    piece_width = width // PIECES

    def columns(factors):
        padded = jnp.concatenate([factors, jnp.zeros((128 - factors.shape[0], 128), jnp.float32)], axis=0)
        return jnp.transpose(padded)

    def start_note(side, hop, part):
        number = (side * 4 + hop) * 2 + part
        copy = pltpu.make_async_remote_copy(
            src_ref=out_stats.at[number], dst_ref=in_stats.at[number],
            send_sem=st_send.at[number], recv_sem=st_recv.at[number],
            device_id=device(dz=1 - 2 * side), device_id_type=MESH,
        )
        copy.start()
        notes[side, hop, part] = copy

    def start_piece(side, hop, part, piece):
        number = (side * 4 + hop) * 2 + part
        lanes = pl.ds(piece * piece_width, piece_width)
        copy = pltpu.make_async_remote_copy(
            src_ref=out_mix.at[number, :, lanes], dst_ref=in_mix.at[number, :, lanes],
            send_sem=mix_send.at[number * PIECES + piece], recv_sem=mix_recv.at[number * PIECES + piece],
            device_id=device(dz=1 - 2 * side), device_id_type=MESH,
        )
        copy.start()
        hops[side, hop, part, piece] = copy

    def forward(hop, parts, merge):
        place = [ORDER.index(4 if hop == 0 else (1 - 2 * side) * (4 - hop)) for side in (0, 1)]
        number = [(side * 4 + hop) * 2 + parts[side] for side in (0, 1)]
        factor = [None, None]
        for side in (0, 1):
            first = parts[side] * half
            stats = own_stats[place[side]]
            if merge:
                notes[side, hop - 1, parts[side]].wait_recv()
                other = in_stats[number[side] - 2]
                top = jnp.maximum(stats[0:1], other[0:1])
                mine, theirs = jnp.exp2(stats[0:1] - top), jnp.exp2(other[0:1] - top)
                peak = stats[2:3] * mine + other[2:3] * theirs
                out_stats[number[side], 0:1, :] = top
                out_stats[number[side], 1:2, :] = stats[1:2] * mine + other[1:2] * theirs
                out_stats[number[side], 2:3, :] = peak
                start_note(side, hop, parts[side])
                shares = [mine * (SPREAD / peak), theirs * (other[2:3] / peak)]
                factor[side] = columns(jnp.concatenate(shares, axis=0))[first:first + half]
            else:
                out_stats[number[side]] = stats
                start_note(side, hop, parts[side])
                factor[side] = SPREAD / peaks[pl.ds(place[side] * span + first, half), :]
        for piece in range(PIECES):
            lanes = pl.ds(piece * piece_width, piece_width)
            for side in (0, 1):
                values = acc[pl.ds(place[side] * span + parts[side] * half, half), lanes] * factor[side][:, 0:1]
                if merge:
                    hops[side, hop - 1, parts[side], piece].wait_recv()
                    other = jnp.log2(in_mix[number[side] - 2, :, lanes].astype(jnp.float32))
                    values = values + other * factor[side][:, 1:2]
                out_mix[number[side], :, lanes] = jnp.exp2(values).astype(jnp.bfloat16)
                start_piece(side, hop, parts[side], piece)

    early = 3 * span
    absorb(score(2, 0, early), 2, 0, early)
    note((0, 1, 2))
    forward(0, (0, 1), False)
    forward(1, (1, 0), False)
    absorb(score(2, early, 5 * span), 2, early, 5 * span)
    note((3, 4, 5, 6, 7))
    forward(1, (0, 1), True)
    for hop in (2, 3):
        forward(hop, (1, 0), True)
        forward(hop, (0, 1), True)

    last = 7 * span
    stats = own_stats[7]
    lane = lax.broadcasted_iota(jnp.int32, (1, 128), 1)
    answer = jnp.zeros((1, 128), jnp.float32)
    for part in (0, 1):
        for side in (0, 1):
            notes[side, 3, part].wait_recv()
        plus, minus = in_stats[6 + part], in_stats[14 + part]
        top = jnp.maximum(stats[0:1], jnp.maximum(plus[0:1], minus[0:1]))
        f0 = jnp.exp2(stats[0:1] - top)
        f1 = jnp.exp2(plus[0:1] - top)
        f2 = jnp.exp2(minus[0:1] - top)
        mass = stats[1:2] * f0 + plus[1:2] * f1 + minus[1:2] * f2
        value = (top + jnp.log2(mass)) * LN2
        answer = jnp.where((lane >= part * half) & (lane < (part + 1) * half), value, answer)
        shares = [f0 / mass, f1 * plus[2:3] / (mass * SPREAD), f2 * minus[2:3] / (mass * SPREAD)]
        factor = columns(jnp.concatenate(shares, axis=0))[part * half:(part + 1) * half]
        for piece in range(PIECES):
            lanes = pl.ds(piece * piece_width, piece_width)
            values = acc[pl.ds(last + part * half, half), lanes] * factor[:, 0:1]
            for side in (0, 1):
                hops[side, 3, part, piece].wait_recv()
                sent = jnp.log2(in_mix[side * 8 + 6 + part, :, lanes].astype(jnp.float32))
                values = values + sent * factor[:, 1 + side:2 + side]
            recon[pl.ds(part * half, half), lanes] = values
    density[...] = answer[:, :span]

    for copy in copies:
        copy.wait_send()
    for group in (siblings, hops, notes):
        for copy in group.values():
            copy.wait_send()


def shards(points):
    span = points.shape[0] // lax.axis_size("col")
    width = points.shape[1]
    half = span // 2
    dma = pltpu.SemaphoreType.DMA
    vmem = pltpu.VMEM
    recon, density = pl.pallas_call(
        functools.partial(kernel, span),
        out_shape=(
            jax.ShapeDtypeStruct((span, width), jnp.float32),
            jax.ShapeDtypeStruct((1, span), jnp.float32),
        ),
        in_specs=[pl.BlockSpec(memory_space=pltpu.HBM)],
        out_specs=(pl.BlockSpec(memory_space=pltpu.VMEM), pl.BlockSpec(memory_space=pltpu.VMEM)),
        scratch_shapes=[
            vmem((32 * span, width), jnp.bfloat16),
            vmem((8 * span, width), jnp.bfloat16),
            vmem((8 * span, width), jnp.float32),
            vmem((8 * span, 128), jnp.float32),
            vmem((8 * span, 128), jnp.float32),
            vmem((8 * span, 128), jnp.float32),
            vmem((8, 8, 128), jnp.float32),
            vmem((16, half, width), jnp.bfloat16),
            vmem((16, half, width), jnp.bfloat16),
            vmem((16, 8, 128), jnp.float32),
            vmem((16, 8, 128), jnp.float32),
            dma((9,)),
            dma((52,)),
            dma((52,)),
            dma((19,)),
            dma((19,)),
            dma((16 * PIECES,)),
            dma((16 * PIECES,)),
            dma((16,)),
            dma((16,)),
        ],
        compiler_params=pltpu.CompilerParams(
            collective_id=0, has_side_effects=True, vmem_limit_bytes=62 * 1024 * 1024
        ),
        cost_estimate=pl.CostEstimate(
            flops=4 * 8 * span * 32 * span * width,
            bytes_accessed=16 * span * width * 2,
            transcendentals=8 * span * 32 * span,
        ),
    )(points)
    return density.reshape(span), recon


def solution(mesh):
    return jax.shard_map(
        shards,
        mesh=mesh,
        in_specs=(P("row", None),),
        out_specs=(P(("row", "col")), P(("row", "col"), None)),
        check_vma=False,
    )
```

```python
import functools
import math

import jax
import jax.numpy as jnp
from jax import lax
from jax.experimental import pallas as pl
from jax.experimental.pallas import tpu as pltpu
from jax.sharding import PartitionSpec as P

MESH = pl.DeviceIdType.MESH
NEG = -1e30
LOG2E = math.log2(math.e)
LN2 = math.log(2.0)

NX, NY, NZ = 4, 4, 8
STEPS = (
    ((0, 0), (1, 0), (-1, 0), (0, 1), (0, -1)),
    ((1, 1), (1, -1), (-1, 1), (-1, -1), (2, 0), (0, 2)),
    ((1, 2), (-1, 2), (2, 1), (2, -1), (2, 2)),
)
PIECES = 2
SPREAD = 120.0
TINY = 1e-30
ORDER = (4, 3, -3, 2, -2, 1, -1, 0)
DIRS = {"x+": (1, 0), "x-": (-1, 0), "y+": (0, 1), "y-": (0, -1)}


def wrap(v):
    v %= 4
    return v - 4 if v == 3 else v


def kernel(span, points, recon, density, keys, queries, acc, tops, sums, peaks, own_stats,
           in_mix, out_mix, in_stats, out_stats,
           load_sem, send_sem, recv_sem, sib_send, sib_recv, mix_send, mix_recv, st_send, st_recv):
    width = points.shape[1]
    half = span // 2
    wide = width // 2
    scale2 = LOG2E / math.sqrt(width)
    row_index, col_index = lax.axis_index("row"), lax.axis_index("col")
    x_hi, y, core = row_index // 8, (row_index // 2) % 4, row_index % 2
    z, x_lo = col_index // 2, col_index % 2
    x = x_hi * 2 + x_lo

    def device(dx=0, dy=0, dz=0, flip=False):
        tx, ty, tz = (x + dx + 4) % 4, (y + dy + 4) % 4, (z + dz + 8) % 8
        tc = 1 - core if flip else core
        return ((tx // 2 * 4 + ty) * 2 + tc, tz * 2 + tx % 2)

    base = {}
    first = []
    total = 0
    for slots in STEPS:
        first.append(total)
        for plane in range(2):
            for slot in slots:
                base[slot, plane] = total
                total += span

    loads = []
    own_rows = pl.ds(pl.multiple_of(col_index * span, span), span)
    own = pltpu.make_async_copy(
        points.at[own_rows], keys.at[pl.ds(base[(0, 0), 0], span)], load_sem.at[0]
    )
    own.start()
    for place, dz in enumerate(ORDER):
        start = pl.multiple_of((((z + dz + 8) % 8) * 2 + x_lo) * span, span)
        load = pltpu.make_async_copy(
            points.at[pl.ds(start, span)], queries.at[pl.ds(place * span, span)], load_sem.at[1 + place]
        )
        load.start()
        loads.append(load)

    barrier = pltpu.get_barrier_semaphore()
    partners = [device(dx=dx, dy=dy) for dx, dy in DIRS.values()]
    partners += [device(dx=dx, dy=dy, flip=True) for dx, dy in DIRS.values()]
    partners += [device(dz=1), device(dz=-1), device(flip=True)]
    for partner in partners:
        pl.semaphore_signal(barrier, inc=1, device_id=partner, device_id_type=MESH)
    pl.semaphore_wait(barrier, len(partners))

    messages, waited, copies = {}, set(), []

    def send(way, slot, part, cols=None, plane=0):
        dx, dy = DIRS[way]
        target = (wrap(slot[0] - dx), wrap(slot[1] - dy))
        offset = 0 if part == "A" else half
        lanes = pl.ds(0, width) if cols is None else pl.ds(cols * wide, wide)
        copy = pltpu.make_async_remote_copy(
            src_ref=keys.at[pl.ds(base[slot, 0] + offset, half), lanes],
            dst_ref=keys.at[pl.ds(base[target, plane] + offset, half), lanes],
            send_sem=send_sem.at[len(copies)],
            recv_sem=recv_sem.at[len(copies)],
            device_id=device(dx=dx, dy=dy, flip=plane == 1),
            device_id_type=MESH,
        )
        copy.start()
        messages.setdefault((target, part, plane), []).append((cols, len(copies)))
        copies.append(copy)

    def send_halves(way, slot, part):
        for cols in ((0, 1) if way in ("x+", "y+") else (1, 0)):
            send(way, slot, part, cols)

    def arrived(slot, part, cols=None, plane=0):
        for held, number in messages[slot, part, plane]:
            if number not in waited and (cols is None or held is None or held == cols):
                waited.add(number)
                copies[number].wait_recv()

    siblings = {}

    def share(slot, part=None):
        number = len(siblings)
        rows = span if part is None else half
        offset = half if part == "B" else 0
        copy = pltpu.make_async_remote_copy(
            src_ref=keys.at[pl.ds(base[slot, 0] + offset, rows)],
            dst_ref=keys.at[pl.ds(base[slot, 1] + offset, rows)],
            send_sem=sib_send.at[number],
            recv_sem=sib_recv.at[number],
            device_id=device(flip=True),
            device_id_type=MESH,
        )
        copy.start()
        siblings[slot, part] = copy

    def score(step, start, rows):
        block = keys[pl.ds(first[step], 2 * len(STEPS[step]) * span), :]
        return lax.dot_general(
            queries[pl.ds(start, rows), :], block, (((1,), (1,)), ((), ())),
            preferred_element_type=jnp.float32,
        )

    def absorb(scores, step, start, rows, masked_from=None):
        mine = pl.ds(start, rows)
        block = keys[pl.ds(first[step], 2 * len(STEPS[step]) * span), :]
        scores = scores * scale2
        if masked_from is not None:
            r = lax.broadcasted_iota(jnp.int32, scores.shape, 0) - masked_from
            c = lax.broadcasted_iota(jnp.int32, scores.shape, 1)
            scores = jnp.where(r == c, NEG, scores)
        top = jnp.max(scores, axis=1, keepdims=True)
        if step > 0:
            before = tops[mine, 0:1]
            top = jnp.maximum(top, before)
            shrink = jnp.exp2(before - top)
        weight = jnp.exp2(scores - top).astype(jnp.bfloat16)
        mass = jnp.sum(weight.astype(jnp.float32), axis=1, keepdims=True)
        mix = jnp.dot(weight, block, preferred_element_type=jnp.float32)
        if step > 0:
            mass = mass + sums[mine, 0:1] * shrink
            mix = mix + acc[mine, :] * shrink
        acc[mine, :] = mix
        tops[mine, :] = jnp.broadcast_to(top, (rows, 128))
        sums[mine, :] = jnp.broadcast_to(mass, (rows, 128))

    own.wait()
    for way in ("x+", "x-"):
        send_halves(way, (0, 0), "A")
    for way in ("y+", "y-"):
        send_halves(way, (0, 0), "B")
    for way in ("x+", "x-"):
        send(way, (0, 0), "B")
    for way in ("y+", "y-"):
        send(way, (0, 0), "A")
    share((0, 0))
    for load in loads:
        load.wait()

    def pass_on(side, part_x, part_y, planes=(0,)):
        for way, slot, part, cols in (
            ("x+", (-1, side), part_x, 0), ("x-", (1, side), part_x, 1),
            ("y+", (side, -1), part_y, 0), ("y-", (side, 1), part_y, 1),
        ):
            arrived(slot, part, cols)
            for plane in planes:
                send(way, slot, part, cols, plane)

    pass_on(0, "A", "B")
    for side in (1, -1):
        arrived((side, 0), "A")
        for way in ("y+", "y-"):
            send(way, (side, 0), "A")
        arrived((0, side), "B")
        for way in ("x+", "x-"):
            send(way, (0, side), "B")
    for slot in STEPS[0][1:]:
        arrived(slot, "A")
        arrived(slot, "B")
        share(slot)
    arrived((2, 0), "A")
    for way in ("y+", "y-"):
        send_halves(way, (2, 0), "A")
    arrived((0, 2), "B")
    for way in ("x+", "x-"):
        send_halves(way, (0, 2), "B")
    pass_on(0, "B", "A")
    for slot in STEPS[0]:
        siblings[slot, None].wait_recv()

    most = 4 * span
    near, far = score(0, 0, most), score(0, most, most)
    pass_on(1, "B", "A")
    absorb(near, 0, 0, most)
    pass_on(-1, "B", "A")
    for slot in STEPS[1][:4]:
        arrived(slot, "A")
        arrived(slot, "B")
        share(slot)
    absorb(far, 0, most, most, masked_from=3 * span)
    pass_on(2, "B", "A", (0, 1))
    for slot in STEPS[1][4:]:
        arrived(slot, "A")
        arrived(slot, "B")
        share(slot)
    for slot in STEPS[1]:
        siblings[slot, None].wait_recv()
    near, far = score(1, 0, most), score(1, most, most)
    for side in (1, -1):
        for part in ("A", "B"):
            arrived((2, side), part)
            share((2, side), part)
            arrived((side, 2), part)
            share((side, 2), part)
    absorb(near, 1, 0, most)
    absorb(far, 1, most, most)
    for part in ("A", "B"):
        for plane in (0, 1):
            arrived((2, 2), part, plane=plane)
    for slot in STEPS[2][:4]:
        for part in ("A", "B"):
            siblings[slot, part].wait_recv()

    def note(places):
        lane = lax.broadcasted_iota(jnp.int32, (span, 128), 1)
        table = jnp.zeros((span, 128), jnp.float32)
        for index, place in enumerate(places):
            mine = pl.ds(place * span, span)
            peak = jnp.maximum(jnp.max(jnp.abs(acc[mine, :]), axis=1, keepdims=True), TINY)
            peaks[mine, :] = jnp.broadcast_to(peak, (span, 128))
            for row, values in enumerate((tops[mine, :], sums[mine, :], peak)):
                table = jnp.where(lane == 3 * index + row, values, table)
        table = jnp.transpose(jnp.concatenate([table, jnp.zeros((128 - span, 128), jnp.float32)], axis=0))
        for index, place in enumerate(places):
            own_stats[place, 0:3, :] = table[3 * index:3 * index + 3]

    hops, notes = {}, {}
    piece_width = width // PIECES

    def columns(factors):
        padded = jnp.concatenate([factors, jnp.zeros((128 - factors.shape[0], 128), jnp.float32)], axis=0)
        return jnp.transpose(padded)

    def start_note(side, hop, part):
        number = (side * 4 + hop) * 2 + part
        copy = pltpu.make_async_remote_copy(
            src_ref=out_stats.at[number], dst_ref=in_stats.at[number],
            send_sem=st_send.at[number], recv_sem=st_recv.at[number],
            device_id=device(dz=1 - 2 * side), device_id_type=MESH,
        )
        copy.start()
        notes[side, hop, part] = copy

    def start_piece(side, hop, part, piece):
        number = (side * 4 + hop) * 2 + part
        lanes = pl.ds(piece * piece_width, piece_width)
        copy = pltpu.make_async_remote_copy(
            src_ref=out_mix.at[number, :, lanes], dst_ref=in_mix.at[number, :, lanes],
            send_sem=mix_send.at[number * PIECES + piece], recv_sem=mix_recv.at[number * PIECES + piece],
            device_id=device(dz=1 - 2 * side), device_id_type=MESH,
        )
        copy.start()
        hops[side, hop, part, piece] = copy

    def forward(hop, parts, merge):
        place = [ORDER.index(4 if hop == 0 else (1 - 2 * side) * (4 - hop)) for side in (0, 1)]
        number = [(side * 4 + hop) * 2 + parts[side] for side in (0, 1)]
        factor = [None, None]
        for side in (0, 1):
            first = parts[side] * half
            stats = own_stats[place[side]]
            if merge:
                notes[side, hop - 1, parts[side]].wait_recv()
                other = in_stats[number[side] - 2]
                top = jnp.maximum(stats[0:1], other[0:1])
                mine, theirs = jnp.exp2(stats[0:1] - top), jnp.exp2(other[0:1] - top)
                peak = stats[2:3] * mine + other[2:3] * theirs
                out_stats[number[side], 0:1, :] = top
                out_stats[number[side], 1:2, :] = stats[1:2] * mine + other[1:2] * theirs
                out_stats[number[side], 2:3, :] = peak
                start_note(side, hop, parts[side])
                shares = [mine * (SPREAD / peak), theirs * (other[2:3] / peak)]
                factor[side] = columns(jnp.concatenate(shares, axis=0))[first:first + half]
            else:
                out_stats[number[side]] = stats
                start_note(side, hop, parts[side])
                factor[side] = SPREAD / peaks[pl.ds(place[side] * span + first, half), :]
        for piece in range(PIECES):
            lanes = pl.ds(piece * piece_width, piece_width)
            for side in (0, 1):
                values = acc[pl.ds(place[side] * span + parts[side] * half, half), lanes] * factor[side][:, 0:1]
                if merge:
                    hops[side, hop - 1, parts[side], piece].wait_recv()
                    other = jnp.log2(in_mix[number[side] - 2, :, lanes].astype(jnp.float32))
                    values = values + other * factor[side][:, 1:2]
                out_mix[number[side], :, lanes] = jnp.exp2(values).astype(jnp.bfloat16)
                start_piece(side, hop, parts[side], piece)

    early = 3 * span
    absorb(score(2, 0, early), 2, 0, early)
    note((0, 1, 2))
    forward(0, (0, 1), False)
    forward(1, (1, 0), False)
    absorb(score(2, early, 5 * span), 2, early, 5 * span)
    note((3, 4, 5, 6, 7))
    forward(1, (0, 1), True)
    for hop in (2, 3):
        forward(hop, (1, 0), True)
        forward(hop, (0, 1), True)

    last = 7 * span
    stats = own_stats[7]
    lane = lax.broadcasted_iota(jnp.int32, (1, 128), 1)
    answer = jnp.zeros((1, 128), jnp.float32)
    for part in (0, 1):
        for side in (0, 1):
            notes[side, 3, part].wait_recv()
        plus, minus = in_stats[6 + part], in_stats[14 + part]
        top = jnp.maximum(stats[0:1], jnp.maximum(plus[0:1], minus[0:1]))
        f0 = jnp.exp2(stats[0:1] - top)
        f1 = jnp.exp2(plus[0:1] - top)
        f2 = jnp.exp2(minus[0:1] - top)
        mass = stats[1:2] * f0 + plus[1:2] * f1 + minus[1:2] * f2
        value = (top + jnp.log2(mass)) * LN2
        answer = jnp.where((lane >= part * half) & (lane < (part + 1) * half), value, answer)
        shares = [f0 / mass, f1 * plus[2:3] / (mass * SPREAD), f2 * minus[2:3] / (mass * SPREAD)]
        factor = columns(jnp.concatenate(shares, axis=0))[part * half:(part + 1) * half]
        for piece in range(PIECES):
            lanes = pl.ds(piece * piece_width, piece_width)
            values = acc[pl.ds(last + part * half, half), lanes] * factor[:, 0:1]
            for side in (0, 1):
                hops[side, 3, part, piece].wait_recv()
                sent = jnp.log2(in_mix[side * 8 + 6 + part, :, lanes].astype(jnp.float32))
                values = values + sent * factor[:, 1 + side:2 + side]
            recon[pl.ds(part * half, half), lanes] = values
    density[...] = answer[:, :span]

    for copy in copies:
        copy.wait_send()
    for group in (siblings, hops, notes):
        for copy in group.values():
            copy.wait_send()


def shards(points):
    span = points.shape[0] // lax.axis_size("col")
    width = points.shape[1]
    half = span // 2
    dma = pltpu.SemaphoreType.DMA
    vmem = pltpu.VMEM
    recon, density = pl.pallas_call(
        functools.partial(kernel, span),
        out_shape=(
            jax.ShapeDtypeStruct((span, width), jnp.float32),
            jax.ShapeDtypeStruct((1, span), jnp.float32),
        ),
        in_specs=[pl.BlockSpec(memory_space=pltpu.HBM)],
        out_specs=(pl.BlockSpec(memory_space=pltpu.VMEM), pl.BlockSpec(memory_space=pltpu.VMEM)),
        scratch_shapes=[
            vmem((32 * span, width), jnp.bfloat16),
            vmem((8 * span, width), jnp.bfloat16),
            vmem((8 * span, width), jnp.float32),
            vmem((8 * span, 128), jnp.float32),
            vmem((8 * span, 128), jnp.float32),
            vmem((8 * span, 128), jnp.float32),
            vmem((8, 8, 128), jnp.float32),
            vmem((16, half, width), jnp.bfloat16),
            vmem((16, half, width), jnp.bfloat16),
            vmem((16, 8, 128), jnp.float32),
            vmem((16, 8, 128), jnp.float32),
            dma((9,)),
            dma((52,)),
            dma((52,)),
            dma((19,)),
            dma((19,)),
            dma((16 * PIECES,)),
            dma((16 * PIECES,)),
            dma((16,)),
            dma((16,)),
        ],
        compiler_params=pltpu.CompilerParams(
            collective_id=0, has_side_effects=True, vmem_limit_bytes=62 * 1024 * 1024
        ),
        cost_estimate=pl.CostEstimate(
            flops=4 * 8 * span * 32 * span * width,
            bytes_accessed=16 * span * width * 2,
            transcendentals=8 * span * 32 * span,
        ),
    )(points)
    return density.reshape(span), recon


def solution(mesh):
    return jax.shard_map(
        shards,
        mesh=mesh,
        in_specs=(P("row", None),),
        out_specs=(P(("row", "col")), P(("row", "col"), None)),
        check_vma=False,
    )
```

```python
import functools
import math

import jax
import jax.numpy as jnp
from jax import lax
from jax.experimental import pallas as pl
from jax.experimental.pallas import tpu as pltpu
from jax.sharding import PartitionSpec as P

MESH = pl.DeviceIdType.MESH
NEG = -1e30
LOG2E = math.log2(math.e)
LN2 = math.log(2.0)

NX, NY, NZ = 4, 4, 8
STEPS = (
    ((0, 0), (1, 0), (-1, 0), (0, 1), (0, -1)),
    ((1, 1), (1, -1), (-1, 1), (-1, -1), (2, 0), (0, 2)),
    ((1, 2), (-1, 2), (2, 1), (2, -1), (2, 2)),
)
PIECES = 2
SPREAD = 120.0
TINY = 1e-30
ORDER = (4, 3, -3, 2, -2, 1, -1, 0)
DIRS = {"x+": (1, 0), "x-": (-1, 0), "y+": (0, 1), "y-": (0, -1)}


def wrap(v):
    v %= 4
    return v - 4 if v == 3 else v


def kernel(span, points, recon, density, keys, queries, acc, tops, sums, peaks, own_stats,
           in_mix, out_mix, in_stats, out_stats,
           load_sem, send_sem, recv_sem, sib_send, sib_recv, mix_send, mix_recv, st_send, st_recv):
    width = points.shape[1]
    half = span // 2
    wide = width // 2
    scale2 = LOG2E / math.sqrt(width)
    row_index, col_index = lax.axis_index("row"), lax.axis_index("col")
    x_hi, y, core = row_index // 8, (row_index // 2) % 4, row_index % 2
    z, x_lo = col_index // 2, col_index % 2
    x = x_hi * 2 + x_lo

    def device(dx=0, dy=0, dz=0, flip=False):
        tx, ty, tz = (x + dx + 4) % 4, (y + dy + 4) % 4, (z + dz + 8) % 8
        tc = 1 - core if flip else core
        return ((tx // 2 * 4 + ty) * 2 + tc, tz * 2 + tx % 2)

    base = {}
    first = []
    total = 0
    for slots in STEPS:
        first.append(total)
        for plane in range(2):
            for slot in slots:
                base[slot, plane] = total
                total += span

    loads = []
    own_rows = pl.ds(pl.multiple_of(col_index * span, span), span)
    own = pltpu.make_async_copy(
        points.at[own_rows], keys.at[pl.ds(base[(0, 0), 0], span)], load_sem.at[0]
    )
    own.start()
    for place, dz in enumerate(ORDER):
        start = pl.multiple_of((((z + dz + 8) % 8) * 2 + x_lo) * span, span)
        load = pltpu.make_async_copy(
            points.at[pl.ds(start, span)], queries.at[pl.ds(place * span, span)], load_sem.at[1 + place]
        )
        load.start()
        loads.append(load)

    barrier = pltpu.get_barrier_semaphore()
    partners = [device(dx=dx, dy=dy) for dx, dy in DIRS.values()]
    partners += [device(dx=dx, dy=dy, flip=True) for dx, dy in DIRS.values()]
    partners += [device(dz=1), device(dz=-1), device(flip=True)]
    for partner in partners:
        pl.semaphore_signal(barrier, inc=1, device_id=partner, device_id_type=MESH)
    pl.semaphore_wait(barrier, len(partners))

    messages, waited, copies = {}, set(), []

    def send(way, slot, part, cols=None, plane=0):
        dx, dy = DIRS[way]
        target = (wrap(slot[0] - dx), wrap(slot[1] - dy))
        offset = 0 if part == "A" else half
        lanes = pl.ds(0, width) if cols is None else pl.ds(cols * wide, wide)
        copy = pltpu.make_async_remote_copy(
            src_ref=keys.at[pl.ds(base[slot, 0] + offset, half), lanes],
            dst_ref=keys.at[pl.ds(base[target, plane] + offset, half), lanes],
            send_sem=send_sem.at[len(copies)],
            recv_sem=recv_sem.at[len(copies)],
            device_id=device(dx=dx, dy=dy, flip=plane == 1),
            device_id_type=MESH,
        )
        copy.start()
        messages.setdefault((target, part, plane), []).append((cols, len(copies)))
        copies.append(copy)

    def send_halves(way, slot, part):
        for cols in ((0, 1) if way in ("x+", "y+") else (1, 0)):
            send(way, slot, part, cols)

    def arrived(slot, part, cols=None, plane=0):
        for held, number in messages[slot, part, plane]:
            if number not in waited and (cols is None or held is None or held == cols):
                waited.add(number)
                copies[number].wait_recv()

    siblings = {}

    def share(slot, part=None):
        number = len(siblings)
        rows = span if part is None else half
        offset = half if part == "B" else 0
        copy = pltpu.make_async_remote_copy(
            src_ref=keys.at[pl.ds(base[slot, 0] + offset, rows)],
            dst_ref=keys.at[pl.ds(base[slot, 1] + offset, rows)],
            send_sem=sib_send.at[number],
            recv_sem=sib_recv.at[number],
            device_id=device(flip=True),
            device_id_type=MESH,
        )
        copy.start()
        siblings[slot, part] = copy

    def score(step, start, rows):
        block = keys[pl.ds(first[step], 2 * len(STEPS[step]) * span), :]
        return lax.dot_general(
            queries[pl.ds(start, rows), :], block, (((1,), (1,)), ((), ())),
            preferred_element_type=jnp.float32,
        )

    def absorb(scores, step, start, rows, masked_from=None):
        mine = pl.ds(start, rows)
        block = keys[pl.ds(first[step], 2 * len(STEPS[step]) * span), :]
        scores = scores * scale2
        if masked_from is not None:
            r = lax.broadcasted_iota(jnp.int32, scores.shape, 0) - masked_from
            c = lax.broadcasted_iota(jnp.int32, scores.shape, 1)
            scores = jnp.where(r == c, NEG, scores)
        top = jnp.max(scores, axis=1, keepdims=True)
        if step > 0:
            before = tops[mine, 0:1]
            top = jnp.maximum(top, before)
            shrink = jnp.exp2(before - top)
        weight = jnp.exp2(scores - top).astype(jnp.bfloat16)
        mass = jnp.sum(weight.astype(jnp.float32), axis=1, keepdims=True)
        mix = jnp.dot(weight, block, preferred_element_type=jnp.float32)
        if step > 0:
            mass = mass + sums[mine, 0:1] * shrink
            mix = mix + acc[mine, :] * shrink
        acc[mine, :] = mix
        tops[mine, :] = jnp.broadcast_to(top, (rows, 128))
        sums[mine, :] = jnp.broadcast_to(mass, (rows, 128))

    own.wait()
    for way in ("x+", "x-"):
        send_halves(way, (0, 0), "A")
    for way in ("y+", "y-"):
        send_halves(way, (0, 0), "B")
    for way in ("x+", "x-"):
        send(way, (0, 0), "B")
    for way in ("y+", "y-"):
        send(way, (0, 0), "A")
    share((0, 0))
    for load in loads:
        load.wait()

    def pass_on(side, part_x, part_y, planes=(0,)):
        for way, slot, part, cols in (
            ("x+", (-1, side), part_x, 0), ("x-", (1, side), part_x, 1),
            ("y+", (side, -1), part_y, 0), ("y-", (side, 1), part_y, 1),
        ):
            arrived(slot, part, cols)
            for plane in planes:
                send(way, slot, part, cols, plane)

    pass_on(0, "A", "B")
    for side in (1, -1):
        arrived((side, 0), "A")
        for way in ("y+", "y-"):
            send(way, (side, 0), "A")
        arrived((0, side), "B")
        for way in ("x+", "x-"):
            send(way, (0, side), "B")
    for slot in STEPS[0][1:]:
        arrived(slot, "A")
        arrived(slot, "B")
        share(slot)
    arrived((2, 0), "A")
    for way in ("y+", "y-"):
        send_halves(way, (2, 0), "A")
    arrived((0, 2), "B")
    for way in ("x+", "x-"):
        send_halves(way, (0, 2), "B")
    pass_on(0, "B", "A")
    for slot in STEPS[0]:
        siblings[slot, None].wait_recv()

    most = 4 * span
    near, far = score(0, 0, most), score(0, most, most)
    pass_on(1, "B", "A")
    absorb(near, 0, 0, most)
    pass_on(-1, "B", "A")
    for slot in STEPS[1][:4]:
        arrived(slot, "A")
        arrived(slot, "B")
        share(slot)
    absorb(far, 0, most, most, masked_from=3 * span)
    pass_on(2, "B", "A", (0, 1))
    for slot in STEPS[1][4:]:
        arrived(slot, "A")
        arrived(slot, "B")
        share(slot)
    for slot in STEPS[1]:
        siblings[slot, None].wait_recv()
    near, far = score(1, 0, most), score(1, most, most)
    for side in (1, -1):
        for part in ("A", "B"):
            arrived((2, side), part)
            share((2, side), part)
            arrived((side, 2), part)
            share((side, 2), part)
    absorb(near, 1, 0, most)
    absorb(far, 1, most, most)
    for part in ("A", "B"):
        for plane in (0, 1):
            arrived((2, 2), part, plane=plane)
    for slot in STEPS[2][:4]:
        for part in ("A", "B"):
            siblings[slot, part].wait_recv()

    def note(places):
        lane = lax.broadcasted_iota(jnp.int32, (span, 128), 1)
        table = jnp.zeros((span, 128), jnp.float32)
        for index, place in enumerate(places):
            mine = pl.ds(place * span, span)
            peak = jnp.maximum(jnp.max(jnp.abs(acc[mine, :]), axis=1, keepdims=True), TINY)
            peaks[mine, :] = jnp.broadcast_to(peak, (span, 128))
            for row, values in enumerate((tops[mine, :], sums[mine, :], peak)):
                table = jnp.where(lane == 3 * index + row, values, table)
        table = jnp.transpose(jnp.concatenate([table, jnp.zeros((128 - span, 128), jnp.float32)], axis=0))
        for index, place in enumerate(places):
            own_stats[place, 0:3, :] = table[3 * index:3 * index + 3]

    hops, notes = {}, {}
    piece_width = width // PIECES

    def columns(factors):
        padded = jnp.concatenate([factors, jnp.zeros((128 - factors.shape[0], 128), jnp.float32)], axis=0)
        return jnp.transpose(padded)

    def start_note(side, hop, part):
        number = (side * 4 + hop) * 2 + part
        copy = pltpu.make_async_remote_copy(
            src_ref=out_stats.at[number], dst_ref=in_stats.at[number],
            send_sem=st_send.at[number], recv_sem=st_recv.at[number],
            device_id=device(dz=1 - 2 * side), device_id_type=MESH,
        )
        copy.start()
        notes[side, hop, part] = copy

    def start_piece(side, hop, part, piece):
        number = (side * 4 + hop) * 2 + part
        lanes = pl.ds(piece * piece_width, piece_width)
        copy = pltpu.make_async_remote_copy(
            src_ref=out_mix.at[number, :, lanes], dst_ref=in_mix.at[number, :, lanes],
            send_sem=mix_send.at[number * PIECES + piece], recv_sem=mix_recv.at[number * PIECES + piece],
            device_id=device(dz=1 - 2 * side), device_id_type=MESH,
        )
        copy.start()
        hops[side, hop, part, piece] = copy

    def forward(hop, parts, merge):
        place = [ORDER.index(4 if hop == 0 else (1 - 2 * side) * (4 - hop)) for side in (0, 1)]
        number = [(side * 4 + hop) * 2 + parts[side] for side in (0, 1)]
        factor = [None, None]
        for side in (0, 1):
            first = parts[side] * half
            stats = own_stats[place[side]]
            if merge:
                notes[side, hop - 1, parts[side]].wait_recv()
                other = in_stats[number[side] - 2]
                top = jnp.maximum(stats[0:1], other[0:1])
                mine, theirs = jnp.exp2(stats[0:1] - top), jnp.exp2(other[0:1] - top)
                peak = stats[2:3] * mine + other[2:3] * theirs
                out_stats[number[side], 0:1, :] = top
                out_stats[number[side], 1:2, :] = stats[1:2] * mine + other[1:2] * theirs
                out_stats[number[side], 2:3, :] = peak
                start_note(side, hop, parts[side])
                shares = [mine * (SPREAD / peak), theirs * (other[2:3] / peak)]
                factor[side] = columns(jnp.concatenate(shares, axis=0))[first:first + half]
            else:
                out_stats[number[side]] = stats
                start_note(side, hop, parts[side])
                factor[side] = SPREAD / peaks[pl.ds(place[side] * span + first, half), :]
        for piece in range(PIECES):
            lanes = pl.ds(piece * piece_width, piece_width)
            for side in (0, 1):
                values = acc[pl.ds(place[side] * span + parts[side] * half, half), lanes] * factor[side][:, 0:1]
                if merge:
                    hops[side, hop - 1, parts[side], piece].wait_recv()
                    other = jnp.log2(in_mix[number[side] - 2, :, lanes].astype(jnp.float32))
                    values = values + other * factor[side][:, 1:2]
                out_mix[number[side], :, lanes] = jnp.exp2(values).astype(jnp.bfloat16)
                start_piece(side, hop, parts[side], piece)

    early = 3 * span
    absorb(score(2, 0, early), 2, 0, early)
    note((0, 1, 2))
    forward(0, (0, 1), False)
    forward(1, (1, 0), False)
    absorb(score(2, early, 5 * span), 2, early, 5 * span)
    forward(1, (0, 1), True)
    note((3, 4, 5, 6, 7))
    for hop in (2, 3):
        forward(hop, (1, 0), True)
        forward(hop, (0, 1), True)

    last = 7 * span
    stats = own_stats[7]
    lane = lax.broadcasted_iota(jnp.int32, (1, 128), 1)
    answer = jnp.zeros((1, 128), jnp.float32)
    final = []
    for part in (0, 1):
        for side in (0, 1):
            notes[side, 3, part].wait_recv()
        plus, minus = in_stats[6 + part], in_stats[14 + part]
        top = jnp.maximum(stats[0:1], jnp.maximum(plus[0:1], minus[0:1]))
        f0 = jnp.exp2(stats[0:1] - top)
        f1 = jnp.exp2(plus[0:1] - top)
        f2 = jnp.exp2(minus[0:1] - top)
        mass = stats[1:2] * f0 + plus[1:2] * f1 + minus[1:2] * f2
        value = (top + jnp.log2(mass)) * LN2
        answer = jnp.where((lane >= part * half) & (lane < (part + 1) * half), value, answer)
        shares = [f0 / mass, f1 * plus[2:3] / (mass * SPREAD), f2 * minus[2:3] / (mass * SPREAD)]
        final.append(columns(jnp.concatenate(shares, axis=0))[part * half:(part + 1) * half])
    for part, factor in enumerate(final):
        for piece in range(PIECES):
            lanes = pl.ds(piece * piece_width, piece_width)
            values = acc[pl.ds(last + part * half, half), lanes] * factor[:, 0:1]
            for side in (0, 1):
                hops[side, 3, part, piece].wait_recv()
                sent = jnp.log2(in_mix[side * 8 + 6 + part, :, lanes].astype(jnp.float32))
                values = values + sent * factor[:, 1 + side:2 + side]
            recon[pl.ds(part * half, half), lanes] = values
    density[...] = answer[:, :span]

    for copy in copies:
        copy.wait_send()
    for group in (siblings, hops, notes):
        for copy in group.values():
            copy.wait_send()


def shards(points):
    span = points.shape[0] // lax.axis_size("col")
    width = points.shape[1]
    half = span // 2
    dma = pltpu.SemaphoreType.DMA
    vmem = pltpu.VMEM
    recon, density = pl.pallas_call(
        functools.partial(kernel, span),
        out_shape=(
            jax.ShapeDtypeStruct((span, width), jnp.float32),
            jax.ShapeDtypeStruct((1, span), jnp.float32),
        ),
        in_specs=[pl.BlockSpec(memory_space=pltpu.HBM)],
        out_specs=(pl.BlockSpec(memory_space=pltpu.VMEM), pl.BlockSpec(memory_space=pltpu.VMEM)),
        scratch_shapes=[
            vmem((32 * span, width), jnp.bfloat16),
            vmem((8 * span, width), jnp.bfloat16),
            vmem((8 * span, width), jnp.float32),
            vmem((8 * span, 128), jnp.float32),
            vmem((8 * span, 128), jnp.float32),
            vmem((8 * span, 128), jnp.float32),
            vmem((8, 8, 128), jnp.float32),
            vmem((16, half, width), jnp.bfloat16),
            vmem((16, half, width), jnp.bfloat16),
            vmem((16, 8, 128), jnp.float32),
            vmem((16, 8, 128), jnp.float32),
            dma((9,)),
            dma((52,)),
            dma((52,)),
            dma((19,)),
            dma((19,)),
            dma((16 * PIECES,)),
            dma((16 * PIECES,)),
            dma((16,)),
            dma((16,)),
        ],
        compiler_params=pltpu.CompilerParams(
            collective_id=0, has_side_effects=True, vmem_limit_bytes=62 * 1024 * 1024
        ),
        cost_estimate=pl.CostEstimate(
            flops=4 * 8 * span * 32 * span * width,
            bytes_accessed=16 * span * width * 2,
            transcendentals=8 * span * 32 * span,
        ),
    )(points)
    return density.reshape(span), recon


def solution(mesh):
    return jax.shard_map(
        shards,
        mesh=mesh,
        in_specs=(P("row", None),),
        out_specs=(P(("row", "col")), P(("row", "col"), None)),
        check_vma=False,
    )
```
